512 devices in a mesh: seq: 16 (over z, core), pipe: 32 (over y, x).
Axes of the slice: x: 4, y: 8, z: 8, core: 2. Of those that a mesh axis runs over, the one named last changes fastest.
Arguments:
- projected: bfloat16 [32, 3, 2048, 4096], P('pipe', None, 'seq'), may hold values from -6 to 6
- short_filter: float32 [32, 3, 3, 4096], P('pipe'), may hold values from -3.5 to 3.5
- decay_rate: float32 [32, 16, 4096], P('pipe'), as said below
- residue: float32 [32, 16, 4096], P('pipe'), may hold values from -1.5 to 1.5
- skip_gain: float32 [32, 4096], P('pipe'), may hold values from -4 to 4
Outputs:
- handed: bfloat16 [32, 2048, 4096], P('pipe', 'seq')
The draws below stay inside these ranges and needn't reach their ends.
Inputs may be any that keep to these rules, and one draw needn't show every extreme that they name: `decay_rate`: every rate lies between 0.2 and 64.
All inputs are finite; a program needn't handle non-finite values.
Results may differ from the reference program's by a relative error of at most 0.01.
Values may be sent and summed in bfloat16 or wider, within the bound.
No kernel may reach another device: no remote copies, remote signals or barrier semaphores. Data moves between devices by JAX's collectives and lax.ppermute only.
A program may use at most 128 MiB of HBM per device.

```python
import jax
import jax.numpy as jnp
from jax import lax

D = 4096
ORDER = 16
TAPS = 3
TOKENS = 2048
SECTIONS = 32


def draw_decay_rate(key, part):
    key = jax.random.fold_in(key, 11)
    pick_key, slow_key, fast_key = jax.random.split(key, 3)
    shape = (SECTIONS, ORDER, D)
    slow_share = 0.5
    slow_rate = 0.2 * jnp.exp(jax.random.uniform(slow_key, shape, jnp.float32) * jnp.log(11.5))
    fast_rate = TOKENS * 1.0 / 48.0 * jnp.exp(jax.random.uniform(fast_key, shape, jnp.float32) * jnp.log(1.5))
    chooser = jax.random.uniform(pick_key, shape, jnp.float32)
    return jnp.where(chooser < slow_share, slow_rate, fast_rate).astype(jnp.float32)


def level_of(stream_key, extent, cuts, least, high):
    loudness = 1.0
    for position, parts in cuts:
        draws = jax.random.uniform(jax.random.fold_in(jax.random.fold_in(stream_key, 6), position), (parts,), jnp.float32, least / len(cuts), high / len(cuts))
        loudness = loudness * jnp.repeat(jnp.exp(draws), extent[position] // parts).reshape((-1,) + (1,) * (len(extent) - 1 - position))
    return loudness


def bell_draw(own_key, extent, width, most, cuts=(), held_as=jnp.bfloat16):
    entries = jax.random.normal(own_key, extent, jnp.float32) * width
    if len(cuts) > 0:
        entries = level_of(own_key, extent, cuts, -0.22, 0.18) * entries
    return jnp.clip(entries, min=-most, max=most).astype(held_as)


def setup_inputs(seed: int = 0) -> dict:
    key_of = jax.random.split(jax.random.key(seed), 6)
    projected = bell_draw(key_of[0], (SECTIONS, 3, TOKENS, D), 1.0, 6.0, ((0, 32), (2, 16)))
    short_filter = bell_draw(key_of[1], (SECTIONS, 3, TAPS, D), TAPS ** -0.5, 3.5, ((0, 32),), jnp.float32)
    decay_rate = draw_decay_rate(jax.random.fold_in(key_of[5], 71), 0)
    residue = bell_draw(key_of[3], (SECTIONS, ORDER, D), ORDER ** -0.5, 1.5, ((0, 32),), jnp.float32)
    skip_gain = bell_draw(key_of[4], (SECTIONS, D), 1.0, 4.0, ((0, 32),), jnp.float32)
    return {"projected": projected, "short_filter": short_filter, "decay_rate": decay_rate, "residue": residue, "skip_gain": skip_gain}


def section_mix(operands):
    inputs_now, taps_now, rates_now, weights_now, skips_now = operands
    length = inputs_now.shape[1]
    padded = jnp.pad(inputs_now.astype(jnp.float32), ((0, 0), (TAPS - 1, 0), (0, 0)))
    featured = taps_now[:, 0, None, :] * padded[:, TAPS - 1:TAPS - 1 + length, :]
    for offset in range(1, TAPS):
        featured = featured + taps_now[:, offset, None, :] * padded[:, TAPS - 1 - offset:TAPS - 1 - offset + length, :]
    gated = (featured[1] * featured[2]).astype(jnp.bfloat16)
    decay = rates_now / TOKENS
    scaled = weights_now * jnp.sqrt(-jnp.expm1(-2.0 * decay))
    moments = jnp.arange(length, dtype=jnp.float32)[:, None]
    kernel = scaled[0] * jnp.exp(-decay[0] * moments)
    for order_index in range(1, ORDER):
        kernel = kernel + scaled[order_index] * jnp.exp(-decay[order_index] * moments)
    spectrum = jnp.fft.rfft(gated.astype(jnp.float32), n=2 * length, axis=0) * jnp.fft.rfft(kernel, n=2 * length, axis=0)
    mixed = jnp.fft.irfft(spectrum, n=2 * length, axis=0)[:length]
    return (featured[0] * (mixed + skips_now * gated.astype(jnp.float32))).astype(jnp.bfloat16)

def reference(projected, short_filter, decay_rate, residue, skip_gain):
    outputs = lax.map(section_mix, (projected, short_filter, decay_rate, residue, skip_gain))
    return jnp.concatenate([jnp.zeros_like(outputs[:1]), outputs[:-1]], axis=0)
```

```python
import functools

import jax
import jax.numpy as jnp
from jax import lax
from jax.experimental import pallas as pl
from jax.experimental.pallas import tpu as pltpu
from jax.sharding import PartitionSpec as P

TAPS = 3
LANES = 128
ROWS = 8
GROUP = ROWS * LANES


def spread_rows(dst, base, pitch, value):
    n = value.shape[0]
    for k in range(ROWS):
        dst[pl.ds(base + k * pitch, n), :] = value[:, k * LANES : (k + 1) * LANES]


def state_kernel(order, length, pitch, total,
                 inputs, rim, taps, rates, end_ref, span_ref, lead_ref, gate_ref,
                 raw, tap_rows, rate_rows):
    f32 = jnp.float32
    for i in range(3):
        for k in range(ROWS):
            lanes = pl.ds(k * LANES, LANES)
            raw[i, pl.ds(k * pitch + 8, length), :] = inputs[0, i, :, lanes].astype(f32)
            raw[i, pl.ds(k * pitch + 8 - (TAPS - 1), TAPS - 1), :] = rim[0, i, :, lanes].astype(f32)
        for a in range(TAPS):
            for k in range(ROWS):
                tap_rows[i, a, pl.ds(k, 1), :] = taps[0, i, pl.ds(a, 1), pl.ds(k * LANES, LANES)]
    for k in range(ROWS):
        rate_rows[pl.ds(k * order, order), :] = rates[0, :, pl.ds(k * LANES, LANES)]

    def token(i, t):
        return raw[i, pl.ds(8 + t, ROWS, stride=pitch), :]

    weights = [[tap_rows[i, a] for a in range(TAPS)] for i in range(3)]

    def feature_step(t, before):
        after = []
        made = []
        for i in range(3):
            now = token(i, t)
            one, two = before[i]
            made.append(weights[i][0] * now + weights[i][1] * one + weights[i][2] * two)
            after.append((now, one))
        lead_ref[0, t] = made[0]
        gate_ref[0, t] = (made[1] * made[2]).astype(jnp.bfloat16).astype(f32)
        return tuple(after)

    lax.fori_loop(0, length, feature_step,
                  tuple((token(i, -1), token(i, -2)) for i in range(3)), unroll=8)

    steps = []
    for n in range(order):
        rate = rate_rows[pl.ds(n, ROWS, stride=order), :]
        span_ref[0, n] = rate * (length / total)
        steps.append(jnp.exp(-(rate / total)))

    def state_step(t, states):
        gated = gate_ref[0, t]
        return tuple(s * x + gated for s, x in zip(steps, states))

    zero = jnp.zeros((ROWS, LANES), f32)
    states = lax.fori_loop(0, length, state_step, (zero,) * order, unroll=4)
    for n in range(order):
        end_ref[0, n] = states[n]


def output_kernel(order, length, pitch, total,
                  lead, gate, rates, scaled, skip, start, out_ref,
                  rows, rate_rows, scale_rows, skip_rows):
    for k in range(ROWS):
        lanes = pl.ds(k * LANES, LANES)
        rate_rows[pl.ds(k * order, order), :] = rates[0, :, lanes]
        scale_rows[pl.ds(k * order, order), :] = scaled[:, lanes]
        skip_rows[pl.ds(k, 1), :] = skip[:, lanes]
    steps, scales = [], []
    for n in range(order):
        steps.append(jnp.exp(-(rate_rows[pl.ds(n, ROWS, stride=order), :] / total)))
        scales.append(scale_rows[pl.ds(n, ROWS, stride=order), :])

    def mix_step(t, states):
        gated = gate[0, t]
        states = tuple(s * x + gated for s, x in zip(steps, states))
        parts = [w * x for w, x in zip(scales, states)]
        while len(parts) > 1:
            parts = [parts[i] + parts[i + 1] for i in range(0, len(parts), 2)]
        made = lead[0, t] * (parts[0] + skip_rows[...] * gated)
        rows[pl.ds(t, ROWS, stride=pitch), :] = made
        return states

    lax.fori_loop(0, length, mix_step, tuple(start[0, n] for n in range(order)), unroll=2)
    for k in range(ROWS):
        out_ref[0, :, pl.ds(k * LANES, LANES)] = rows[pl.ds(k * pitch, length), :].astype(jnp.bfloat16)


def local_states(projected, rim, short_filter, decay_rate, total):
    length, width = projected.shape[2:]
    order = decay_rate.shape[1]
    groups = width // GROUP
    pitch = length + 8
    f32 = jnp.float32
    whole = lambda n: pl.BlockSpec((1, n, ROWS, LANES), lambda g: (g, 0, 0, 0))
    shape = lambda n: jax.ShapeDtypeStruct((groups, n, ROWS, LANES), f32)
    return pl.pallas_call(
        functools.partial(state_kernel, order, length, pitch, total),
        grid=(groups,),
        in_specs=[
            pl.BlockSpec((1, 3, length, GROUP), lambda g: (0, 0, 0, g)),
            pl.BlockSpec((1, 3, TAPS - 1, GROUP), lambda g: (0, 0, 0, g)),
            pl.BlockSpec((1, 3, TAPS, GROUP), lambda g: (0, 0, 0, g)),
            pl.BlockSpec((1, order, GROUP), lambda g: (0, 0, g)),
        ],
        out_specs=[whole(order), whole(order), whole(length), whole(length)],
        out_shape=[shape(order), shape(order), shape(length), shape(length)],
        scratch_shapes=[
            pltpu.VMEM((3, ROWS * pitch, LANES), f32),
            pltpu.VMEM((3, TAPS, ROWS, LANES), f32),
            pltpu.VMEM((ROWS * order, LANES), f32),
        ],
        compiler_params=pltpu.CompilerParams(vmem_limit_bytes=24 << 20),
        name="local_states",
    )(projected, rim, short_filter, decay_rate)


def mixed_output(lead, gate, decay_rate, scaled, skip_gain, start, total):
    groups, length = lead.shape[:2]
    order = decay_rate.shape[1]
    pitch = length
    f32 = jnp.float32
    whole = lambda n: pl.BlockSpec((1, n, ROWS, LANES), lambda g: (g, 0, 0, 0))
    return pl.pallas_call(
        functools.partial(output_kernel, order, length, pitch, total),
        grid=(groups,),
        in_specs=[
            whole(length),
            whole(length),
            pl.BlockSpec((1, order, GROUP), lambda g: (0, 0, g)),
            pl.BlockSpec((order, GROUP), lambda g: (0, g)),
            pl.BlockSpec((1, GROUP), lambda g: (0, g)),
            whole(order),
        ],
        out_specs=pl.BlockSpec((1, length, GROUP), lambda g: (0, 0, g)),
        out_shape=jax.ShapeDtypeStruct((1, length, groups * GROUP), jnp.bfloat16),
        scratch_shapes=[
            pltpu.VMEM((ROWS * pitch, LANES), f32),
            pltpu.VMEM((ROWS * order, LANES), f32),
            pltpu.VMEM((ROWS * order, LANES), f32),
            pltpu.VMEM((ROWS, LANES), f32),
        ],
        compiler_params=pltpu.CompilerParams(vmem_limit_bytes=24 << 20),
        name="mixed_output",
    )(lead, gate, decay_rate, scaled, skip_gain, start)


def moved(x, pairs):
    return lax.ppermute(x, "seq", pairs)


def prefix(ends, span):
    nseq = lax.axis_size("seq")
    chips = nseq // 2
    me = lax.axis_index("seq")
    core, chip = me % 2, me // 2
    half = ends.shape[1] // 2
    first = core == 0
    low = lambda x: x[:, :half]
    high = lambda x: x[:, half:]
    mine = lambda x: jnp.where(first, low(x), high(x))
    others = lambda x: jnp.where(first, high(x), low(x))
    swap = [(i, i ^ 1) for i in range(nseq)]
    own, came = mine(ends), moved(others(ends), swap)
    span = mine(span)
    zeroth, oneth = jnp.where(first, own, came), jnp.where(first, came, own)
    fade = jnp.exp(-span)
    whole = fade * zeroth + oneth
    enter = None
    step = 1
    while step < chips // 2:
        came = moved(whole, [(i, ((i // 2) ^ step) * 2 + i % 2) for i in range(nseq)])
        right = (chip & step) != 0
        far = jnp.exp(-span * (2 * (chip & (step - 1))).astype(jnp.float32))
        into = jnp.where(right, far * came, 0.0)
        enter = into if enter is None else enter + into
        fading = jnp.exp(-span * (2.0 * step))
        whole = jnp.where(right, fading * came + whole, fading * whole + came)
        step *= 2
    came = moved(whole, [(c * 2 + k, (chips - 1 - c) * 2 + k) for c in range(chips // 2) for k in range(2)])
    far = jnp.exp(-span * (2 * (chip & (step - 1))).astype(jnp.float32))
    enter = enter + far * came
    second = fade * enter + zeroth
    came = moved(jnp.where(first, second, enter), swap)
    own = jnp.where(first, enter, second)
    return jnp.concatenate([jnp.where(first, own, came), jnp.where(first, came, own)], axis=1)


def shards(projected, short_filter, decay_rate, residue, skip_gain):
    length = projected.shape[2]
    nseq = lax.axis_size("seq")
    total = length * nseq
    edge = projected[:, :, length - (TAPS - 1) :, :]
    rim = moved(edge, [(i, i + 1) for i in range(nseq - 1)])
    ends, span, lead, gate = local_states(projected, rim, short_filter, decay_rate, total)
    scaled = residue[0] * jnp.sqrt(-jnp.expm1(-2.0 * (decay_rate[0] / total)))
    start = prefix(ends, span)
    output = mixed_output(lead, gate, decay_rate, scaled, skip_gain, start, total)
    sections = lax.axis_size("pipe")
    return lax.ppermute(output, "pipe", [(i, i + 1) for i in range(sections - 1)])


def solution(mesh):
    in_specs = (
        P("pipe", None, "seq", None),
        P("pipe", None, None, None),
        P("pipe", None, None),
        P("pipe", None, None),
        P("pipe", None),
    )
    out_specs = P("pipe", "seq", None)
    return jax.shard_map(shards, mesh=mesh, in_specs=in_specs, out_specs=out_specs, check_vma=False)
```

```python
import functools

import jax
import jax.numpy as jnp
from jax import lax
from jax.experimental import pallas as pl
from jax.experimental.pallas import tpu as pltpu
from jax.sharding import PartitionSpec as P

TAPS = 3
LANES = 128
ROWS = 8
GROUP = ROWS * LANES


def spread_rows(dst, base, pitch, value):
    n = value.shape[0]
    for k in range(ROWS):
        dst[pl.ds(base + k * pitch, n), :] = value[:, k * LANES : (k + 1) * LANES]


def state_kernel(order, length, pitch, total,
                 inputs, rim, taps, rates, end_ref, span_ref, lead_ref, gate_ref,
                 raw, tap_rows, rate_rows):
    f32 = jnp.float32
    for i in range(3):
        for k in range(ROWS):
            lanes = pl.ds(k * LANES, LANES)
            raw[i, pl.ds(k * pitch + 8, length), :] = inputs[0, i, :, lanes].astype(f32)
            raw[i, pl.ds(k * pitch + 8 - (TAPS - 1), TAPS - 1), :] = rim[0, i, :, lanes].astype(f32)
        for a in range(TAPS):
            for k in range(ROWS):
                tap_rows[i, a, pl.ds(k, 1), :] = taps[0, i, pl.ds(a, 1), pl.ds(k * LANES, LANES)]
    for k in range(ROWS):
        rate_rows[pl.ds(k * order, order), :] = rates[0, :, pl.ds(k * LANES, LANES)]

    def token(i, t):
        return raw[i, pl.ds(8 + t, ROWS, stride=pitch), :]

    weights = [[tap_rows[i, a] for a in range(TAPS)] for i in range(3)]

    def feature_step(t, before):
        after = []
        made = []
        for i in range(3):
            now = token(i, t)
            one, two = before[i]
            made.append(weights[i][0] * now + weights[i][1] * one + weights[i][2] * two)
            after.append((now, one))
        lead_ref[0, t] = made[0]
        gate_ref[0, t] = (made[1] * made[2]).astype(jnp.bfloat16).astype(f32)
        return tuple(after)

    lax.fori_loop(0, length, feature_step,
                  tuple((token(i, -1), token(i, -2)) for i in range(3)), unroll=8)

    steps = []
    for n in range(order):
        rate = rate_rows[pl.ds(n, ROWS, stride=order), :]
        span_ref[0, n] = rate * (length / total)
        steps.append(jnp.exp(-(rate / total)))

    def state_step(t, states):
        gated = gate_ref[0, t]
        return tuple(s * x + gated for s, x in zip(steps, states))

    zero = jnp.zeros((ROWS, LANES), f32)
    states = lax.fori_loop(0, length, state_step, (zero,) * order, unroll=4)
    for n in range(order):
        end_ref[0, n] = states[n]


def output_kernel(order, length, pitch, total,
                  lead, gate, rates, scaled, skip, start, out_ref,
                  rows, rate_rows, scale_rows, skip_rows):
    for k in range(ROWS):
        lanes = pl.ds(k * LANES, LANES)
        rate_rows[pl.ds(k * order, order), :] = rates[0, :, lanes]
        scale_rows[pl.ds(k * order, order), :] = scaled[:, lanes]
        skip_rows[pl.ds(k, 1), :] = skip[:, lanes]
    steps, scales = [], []
    for n in range(order):
        steps.append(jnp.exp(-(rate_rows[pl.ds(n, ROWS, stride=order), :] / total)))
        scales.append(scale_rows[pl.ds(n, ROWS, stride=order), :])

    def mix_step(t, states):
        gated = gate[0, t]
        states = tuple(s * x + gated for s, x in zip(steps, states))
        parts = [w * x for w, x in zip(scales, states)]
        while len(parts) > 1:
            parts = [parts[i] + parts[i + 1] for i in range(0, len(parts), 2)]
        made = lead[0, t] * (parts[0] + skip_rows[...] * gated)
        rows[pl.ds(t, ROWS, stride=pitch), :] = made
        return states

    lax.fori_loop(0, length, mix_step, tuple(start[0, n] for n in range(order)), unroll=2)
    for k in range(ROWS):
        out_ref[0, :, pl.ds(k * LANES, LANES)] = rows[pl.ds(k * pitch, length), :].astype(jnp.bfloat16)


def local_states(projected, rim, short_filter, decay_rate, total):
    length, width = projected.shape[2:]
    order = decay_rate.shape[1]
    groups = width // GROUP
    pitch = length + 8
    f32 = jnp.float32
    whole = lambda n: pl.BlockSpec((1, n, ROWS, LANES), lambda g: (g, 0, 0, 0))
    shape = lambda n: jax.ShapeDtypeStruct((groups, n, ROWS, LANES), f32)
    return pl.pallas_call(
        functools.partial(state_kernel, order, length, pitch, total),
        grid=(groups,),
        in_specs=[
            pl.BlockSpec((1, 3, length, GROUP), lambda g: (0, 0, 0, g)),
            pl.BlockSpec((1, 3, TAPS - 1, GROUP), lambda g: (0, 0, 0, g)),
            pl.BlockSpec((1, 3, TAPS, GROUP), lambda g: (0, 0, 0, g)),
            pl.BlockSpec((1, order, GROUP), lambda g: (0, 0, g)),
        ],
        out_specs=[whole(order), whole(order), whole(length), whole(length)],
        out_shape=[shape(order), shape(order), shape(length), shape(length)],
        scratch_shapes=[
            pltpu.VMEM((3, ROWS * pitch, LANES), f32),
            pltpu.VMEM((3, TAPS, ROWS, LANES), f32),
            pltpu.VMEM((ROWS * order, LANES), f32),
        ],
        compiler_params=pltpu.CompilerParams(vmem_limit_bytes=24 << 20),
        name="local_states",
    )(projected, rim, short_filter, decay_rate)


def mixed_output(lead, gate, decay_rate, scaled, skip_gain, start, total):
    groups, length = lead.shape[:2]
    order = decay_rate.shape[1]
    pitch = length
    f32 = jnp.float32
    whole = lambda n: pl.BlockSpec((1, n, ROWS, LANES), lambda g: (g, 0, 0, 0))
    return pl.pallas_call(
        functools.partial(output_kernel, order, length, pitch, total),
        grid=(groups,),
        in_specs=[
            whole(length),
            whole(length),
            pl.BlockSpec((1, order, GROUP), lambda g: (0, 0, g)),
            pl.BlockSpec((order, GROUP), lambda g: (0, g)),
            pl.BlockSpec((1, GROUP), lambda g: (0, g)),
            whole(order),
        ],
        out_specs=pl.BlockSpec((1, length, GROUP), lambda g: (0, 0, g)),
        out_shape=jax.ShapeDtypeStruct((1, length, groups * GROUP), jnp.bfloat16),
        scratch_shapes=[
            pltpu.VMEM((ROWS * pitch, LANES), f32),
            pltpu.VMEM((ROWS * order, LANES), f32),
            pltpu.VMEM((ROWS * order, LANES), f32),
            pltpu.VMEM((ROWS, LANES), f32),
        ],
        compiler_params=pltpu.CompilerParams(vmem_limit_bytes=24 << 20),
        name="mixed_output",
    )(lead, gate, decay_rate, scaled, skip_gain, start)


def moved(x, pairs):
    return lax.ppermute(x, "seq", pairs)


def carried(x, pairs):
    return moved(x.astype(jnp.bfloat16), pairs).astype(jnp.float32)


def prefix(ends, span):
    nseq = lax.axis_size("seq")
    chips = nseq // 2
    me = lax.axis_index("seq")
    core, chip = me % 2, me // 2
    half = ends.shape[1] // 2
    first = core == 0
    low = lambda x: x[:, :half]
    high = lambda x: x[:, half:]
    mine = lambda x: jnp.where(first, low(x), high(x))
    others = lambda x: jnp.where(first, high(x), low(x))
    swap = [(i, i ^ 1) for i in range(nseq)]
    own, came = mine(ends), carried(others(ends), swap)
    span = mine(span)
    zeroth, oneth = jnp.where(first, own, came), jnp.where(first, came, own)
    fade = jnp.exp(-span)
    whole = fade * zeroth + oneth
    enter = None
    step = 1
    while step < chips // 2:
        came = carried(whole, [(i, ((i // 2) ^ step) * 2 + i % 2) for i in range(nseq)])
        right = (chip & step) != 0
        far = jnp.exp(-span * (2 * (chip & (step - 1))).astype(jnp.float32))
        into = jnp.where(right, far * came, 0.0)
        enter = into if enter is None else enter + into
        fading = jnp.exp(-span * (2.0 * step))
        whole = jnp.where(right, fading * came + whole, fading * whole + came)
        step *= 2
    came = carried(whole, [(c * 2 + k, (chips - 1 - c) * 2 + k) for c in range(chips // 2) for k in range(2)])
    far = jnp.exp(-span * (2 * (chip & (step - 1))).astype(jnp.float32))
    enter = enter + far * came
    second = fade * enter + zeroth
    came = carried(jnp.where(first, second, enter), swap)
    own = jnp.where(first, enter, second)
    return jnp.concatenate([jnp.where(first, own, came), jnp.where(first, came, own)], axis=1)


def shards(projected, short_filter, decay_rate, residue, skip_gain):
    length = projected.shape[2]
    nseq = lax.axis_size("seq")
    total = length * nseq
    edge = projected[:, :, length - (TAPS - 1) :, :]
    rim = moved(edge, [(i, i + 1) for i in range(nseq - 1)])
    ends, span, lead, gate = local_states(projected, rim, short_filter, decay_rate, total)
    scaled = residue[0] * jnp.sqrt(-jnp.expm1(-2.0 * (decay_rate[0] / total)))
    start = prefix(ends, span)
    output = mixed_output(lead, gate, decay_rate, scaled, skip_gain, start, total)
    sections = lax.axis_size("pipe")
    return lax.ppermute(output, "pipe", [(i, i + 1) for i in range(sections - 1)])


def solution(mesh):
    in_specs = (
        P("pipe", None, "seq", None),
        P("pipe", None, None, None),
        P("pipe", None, None),
        P("pipe", None, None),
        P("pipe", None),
    )
    out_specs = P("pipe", "seq", None)
    return jax.shard_map(shards, mesh=mesh, in_specs=in_specs, out_specs=out_specs, check_vma=False)
```

```python
import functools

import jax
import jax.numpy as jnp
from jax import lax
from jax.experimental import pallas as pl
from jax.experimental.pallas import tpu as pltpu
from jax.sharding import PartitionSpec as P

TAPS = 3
LANES = 128
ROWS = 8
GROUP = ROWS * LANES
PARTS = 2
PLACE_OPS = 10000
f32 = jnp.float32
bf16 = jnp.bfloat16


def tree_sum(parts):
    while len(parts) > 1:
        parts = [parts[i] + parts[i + 1] for i in range(0, len(parts), 2)]
    return parts[0]


def by_mode(rows, values, order):
    for k in range(ROWS):
        rows[pl.ds(k * order, order), :] = values[:, k * LANES : (k + 1) * LANES]
    return [rows[pl.ds(n, ROWS, stride=order), :] for n in range(order)]


def state_kernel(order, length, pitch, total,
                 inputs, tap_source, rate_source, end_ref, span_ref, head, gate,
                 held_inputs, taps, rates, raw, mode_rows, sems):
    groups = held_inputs.shape[0]

    def fetch(g):
        return pltpu.make_async_copy(
            inputs.at[0, pl.ds(1, 2), :, pl.ds(g * GROUP, GROUP)], held_inputs.at[g], sems.at[g]
        )

    tap_copy = pltpu.make_async_copy(tap_source, taps, sems.at[groups])
    rate_copy = pltpu.make_async_copy(rate_source.at[0], rates, sems.at[groups + 1])
    fetch(0).start()
    tap_copy.start()
    rate_copy.start()
    for g in range(1, groups):
        fetch(g).start()
    zero = jnp.zeros((ROWS, LANES), f32)

    for g in range(groups):
        at = pl.ds(g * ROWS, ROWS)
        fetch(g).wait()
        for i in range(2):
            for k in range(ROWS):
                raw[i, pl.ds(k * pitch + 8, length), :] = held_inputs[g, i, :, k * LANES : (k + 1) * LANES].astype(f32)
        if g == 0:
            tap_copy.wait()
            rate_copy.wait()

        def token(i, t):
            return raw[i, pl.ds(8 + t, ROWS, stride=pitch), :]

        weights = [[taps[TAPS * (1 + i) + a, at, :] for a in range(TAPS)] for i in range(2)]

        def features(t, before):
            after, made = [], []
            for i in range(2):
                now = token(i, t)
                one, two = before[i]
                made.append(weights[i][0] * now + weights[i][1] * one + weights[i][2] * two)
                after.append((now, one))
            return tuple(after), made

        def feature_step(pair, before):
            gates = []
            for sub in range(2):
                before, made = features(2 * pair + sub, before)
                gates.append(made[0] * made[1])
            gate[g, pair] = jnp.concatenate(gates, axis=0).astype(bf16)
            return before

        before = ((zero, zero),) * 2
        for t in range(TAPS - 1):
            before, made = features(t, before)
            for i in range(2):
                head[2 * i + t, at, :] = made[i]
        lax.fori_loop(1, length // 2, feature_step, before, unroll=9)

        steps = []
        for n, rate in enumerate(by_mode(mode_rows, rates[:, g * GROUP : (g + 1) * GROUP], order)):
            span_ref[n, at, :] = rate * (length / total)
            steps.append(jnp.exp(-(rate / total)))

        def state_step(pair, states):
            both = gate[g, pair].astype(f32)
            for sub in range(2):
                gated = both[sub * ROWS : (sub + 1) * ROWS]
                states = tuple(s * x + gated for s, x in zip(steps, states))
            return states

        states = lax.fori_loop(1, length // 2, state_step, (zero,) * order, unroll=3)
        for n in range(order):
            end_ref[n, at, :] = states[n]


def patch_kernel(order, length, rim, head, taps, ends, span, wire, edge, rows):
    tiles = ends.shape[1]
    for i in range(3):
        came = rim[0, i].astype(f32)
        for t in range(TAPS - 1):
            for k in range(tiles):
                rows[2 * i + t, pl.ds(k, 1), :] = came[t : t + 1, k * LANES : (k + 1) * LANES]
    edge[0] = rows[0]
    edge[1] = rows[1]
    made = []
    for i in range(1, 3):
        two, one = rows[2 * i], rows[2 * i + 1]
        made.append((head[2 * i - 2] + taps[TAPS * i + 1] * one + taps[TAPS * i + 2] * two,
                     head[2 * i - 1] + taps[TAPS * i + 2] * one))
    gated = []
    for t in range(2):
        gated.append((made[0][t] * made[1][t]).astype(bf16).astype(f32))
        edge[2 + t] = gated[t]
    for n in range(order):
        step = span[n] * (1.0 / length)
        first = jnp.exp(-step) * gated[0] + gated[1]
        wire[n] = (ends[n] + jnp.exp(-(length - 2) * step) * first).astype(bf16)


def mix_kernel(order, length, pitch, total, inputs, taps, gate, edge, rates, scaled, skip, lead, mix, raw, mode_rows):
    steps = [jnp.exp(-(rate / total)) for rate in by_mode(mode_rows, rates[0], order)]
    scales = by_mode(mode_rows, scaled[...], order)
    weights = [taps[a] for a in range(TAPS)]
    for k in range(ROWS):
        raw[pl.ds(k * pitch, length), :] = inputs[0, 0, :, k * LANES : (k + 1) * LANES].astype(f32)

    def lead_step(pair, before):
        for sub in range(2):
            t = 2 * pair + sub
            one, two = before
            now = raw[pl.ds(t, ROWS, stride=pitch), :]
            lead[0, t] = weights[0] * now + weights[1] * one + weights[2] * two
            before = (now, one)
        return before

    lax.fori_loop(0, length // 2, lead_step, (edge[1], edge[0]), unroll=4)

    def tokens(pair, states, both):
        for sub, gated in enumerate(both):
            states = tuple(s * x + gated for s, x in zip(steps, states))
            mix[0, 2 * pair + sub] = tree_sum([w * x for w, x in zip(scales, states)]) + skip[...] * gated
        return states

    def step(pair, states):
        both = gate[0, pair].astype(f32)
        return tokens(pair, states, (both[:ROWS], both[ROWS:]))

    states = tokens(0, (jnp.zeros((ROWS, LANES), f32),) * order, (edge[2], edge[3]))
    lax.fori_loop(1, length // 2, step, states)


def finish_kernel(order, length, total, lead, mix, rates, scaled, start, out_ref, rows, mode_rows, start_rows):
    steps = [jnp.exp(-(rate / total)) for rate in by_mode(mode_rows, rates[0], order)]
    scales = by_mode(mode_rows, scaled[...], order)
    start_rows[...] = start[...].astype(f32)
    at = pl.ds(pl.multiple_of(pl.program_id(0) * ROWS, ROWS), ROWS)

    def step(t, terms):
        terms = tuple(s * x for s, x in zip(steps, terms))
        rows[pl.ds(t, ROWS, stride=length), :] = lead[0, t] * (mix[0, t] + tree_sum(list(terms)))
        return terms

    lax.fori_loop(0, length, step, tuple(scales[n] * start_rows[n, at, :] for n in range(order)), unroll=4)
    for k in range(ROWS):
        out_ref[0, :, pl.ds(k * LANES, LANES)] = rows[pl.ds(k * length, length), :].astype(bf16)


def place_kernel(part, *rest):
    rest[-1][...] = part[...]


def scan_kernel(came, span, enter):
    keep = jnp.exp(-span[lax.axis_index("seq")])
    state = jnp.zeros(keep.shape, f32)
    for j in range(came.shape[0]):
        enter[j] = state.astype(bf16)
        state = keep * state + came[j].astype(f32)


def after(*arrays):
    return lax.optimization_barrier(arrays)


def call(body, name, groups, ops, length, in_specs, out_specs, out_shape, scratch, aliases={}):
    return pl.pallas_call(
        body,
        grid=(groups,),
        in_specs=in_specs,
        out_specs=out_specs,
        out_shape=out_shape,
        scratch_shapes=scratch,
        input_output_aliases=aliases,
        compiler_params=pltpu.CompilerParams(vmem_limit_bytes=16 << 20),
        cost_estimate=pl.CostEstimate(
            flops=ops * length * groups * GROUP, bytes_accessed=8 * length * groups * GROUP, transcendentals=0
        ),
        name=name,
    )


def shards(projected, short_filter, decay_rate, residue, skip_gain):
    length, width = projected.shape[2:]
    order = decay_rate.shape[1]
    nseq = lax.axis_size("seq")
    sections = lax.axis_size("pipe")
    total = length * nseq
    groups = width // GROUP
    tiles = width // LANES
    pitch = length + 8
    onward = [(i, i + 1) for i in range(sections - 1)]
    held = lambda x: pltpu.with_memory_space_constraint(x, pltpu.HBM)
    to_all = lambda x: lax.all_to_all(x, "seq", 0, 0, tiled=True)
    taps = short_filter.reshape(3 * TAPS, tiles, LANES)
    skip = skip_gain.reshape(tiles, LANES)
    rim = lax.ppermute(projected[:, :, length - (TAPS - 1) :, :], "seq", [(i, i + 1) for i in range(nseq - 1)])

    tokens = lambda at: pl.BlockSpec((1, length, ROWS, LANES), lambda g: (at + g, 0, 0, 0))
    pairs = lambda at: pl.BlockSpec((1, length // 2, 2 * ROWS, LANES), lambda g: (at + g, 0, 0, 0))
    stack = lambda n, at: pl.BlockSpec((n, ROWS, LANES), lambda g: (0, at + g, 0))
    rate_block = lambda at: pl.BlockSpec((1, order, GROUP), lambda g: (0, 0, at + g))
    scale_block = lambda at: pl.BlockSpec((order, GROUP), lambda g: (0, at + g))
    out_block = lambda at: pl.BlockSpec((1, length, GROUP), lambda g: (0, 0, at + g))
    anywhere = pl.BlockSpec(memory_space=pl.ANY)
    shape = lambda *dims: jax.ShapeDtypeStruct(dims, f32)
    mode_rows = pltpu.VMEM((ROWS * order, LANES), f32)
    ends, span, head, gate = pl.pallas_call(
        functools.partial(state_kernel, order, length, pitch, total),
        in_specs=[anywhere] * 3,
        out_shape=[
            shape(order, tiles, LANES), shape(order, tiles, LANES), shape(4, tiles, LANES),
            jax.ShapeDtypeStruct((groups, length // 2, 2 * ROWS, LANES), bf16),
        ],
        scratch_shapes=[
            pltpu.VMEM((groups, 2, length, GROUP), bf16),
            pltpu.VMEM((3 * TAPS, tiles, LANES), f32),
            pltpu.VMEM((order, width), f32),
            pltpu.VMEM((2, ROWS * pitch, LANES), f32),
            mode_rows,
            pltpu.SemaphoreType.DMA((groups + 2,)),
        ],
        compiler_params=pltpu.CompilerParams(vmem_limit_bytes=16 << 20),
        cost_estimate=pl.CostEstimate(flops=55 * length * width, bytes_accessed=8 * length * width, transcendentals=0),
        name="local_states",
    )(held(projected), held(taps), held(decay_rate))
    wire, edge = pl.pallas_call(
        functools.partial(patch_kernel, order, length),
        out_shape=[jax.ShapeDtypeStruct((order, tiles, LANES), bf16), shape(4, tiles, LANES)],
        scratch_shapes=[pltpu.VMEM((6, tiles, LANES), f32)],
        compiler_params=pltpu.CompilerParams(vmem_limit_bytes=8 << 20),
        name="first_tokens",
    )(rim, head, taps, ends, span)

    share = groups // PARTS

    def local_mix(part, gated):
        at = part * share
        return call(
            functools.partial(mix_kernel, order, length, length, total), "local_mix", share, 80, length,
            [pl.BlockSpec((1, 1, length, GROUP), lambda g: (0, 0, 0, at + g)), stack(TAPS, at),
             pairs(at), stack(4, at), rate_block(at), scale_block(at),
             pl.BlockSpec((ROWS, LANES), lambda g: (at + g, 0))],
            [tokens(0), tokens(0)], [pltpu.HBM((share, length, ROWS, LANES), f32)] * 2,
            [pltpu.VMEM((ROWS * length, LANES), f32), mode_rows],
        )(held(projected), held(taps), gated, edge, held(decay_rate), scaled, held(skip))

    mixes = [None] * PARTS
    wire, gate, residue = after(wire, gate, residue)
    scaled = residue[0] * jnp.sqrt(-jnp.expm1(-2.0 * (decay_rate[0] / total)))
    came = to_all(wire)
    mixes[0] = local_mix(0, gate)
    came, mixes[0], gate = after(came, mixes[0], gate)
    enter = pl.pallas_call(
        scan_kernel,
        out_shape=jax.ShapeDtypeStruct(came.shape, bf16),
        compiler_params=pltpu.CompilerParams(vmem_limit_bytes=4 << 20),
        name="scan_chunks",
    )(came, span)
    enter, gate = after(enter, gate)
    start = to_all(enter)
    mixes[1] = local_mix(1, gate)
    start, mixes[1] = after(start, mixes[1])
    handed = None
    for part in range(PARTS):
        at = part * share
        output = call(
            functools.partial(finish_kernel, order, length, total), "finished", share, 40, length,
            [tokens(0), tokens(0), rate_block(at), scale_block(at),
             pl.BlockSpec((order, share * ROWS, LANES), lambda g, part=part: (0, part, 0))],
            out_block(0), jax.ShapeDtypeStruct((1, length, share * GROUP), bf16),
            [pltpu.VMEM((ROWS * length, LANES), f32), mode_rows, pltpu.VMEM((order, share * ROWS, LANES), f32)],
        )(*map(held, mixes[part]), decay_rate, scaled, start)
        came = lax.ppermute(output, "pipe", onward)
        given = [came] if handed is None else [came, handed]
        handed = call(
            place_kernel, "placed", share, PLACE_OPS, length, [out_block(0)] + [anywhere] * (len(given) - 1),
            out_block(at), jax.ShapeDtypeStruct((1, length, width), bf16), [], {1: 0} if len(given) > 1 else {},
        )(*given)
    return handed


def solution(mesh):
    in_specs = (
        P("pipe", None, "seq", None),
        P("pipe", None, None, None),
        P("pipe", None, None),
        P("pipe", None, None),
        P("pipe", None),
    )
    out_specs = P("pipe", "seq", None)
    return jax.shard_map(shards, mesh=mesh, in_specs=in_specs, out_specs=out_specs, check_vma=False)
```

```python
import functools

import jax
import jax.numpy as jnp
from jax import lax
from jax.experimental import pallas as pl
from jax.experimental.pallas import tpu as pltpu
from jax.sharding import PartitionSpec as P

TAPS = 3
LANES = 128
ROWS = 8
GROUP = ROWS * LANES
EARLY = 2
PLACE_OPS = 10000
PIECES = 4
f32 = jnp.float32
bf16 = jnp.bfloat16


def tree_sum(parts):
    while len(parts) > 1:
        parts = [parts[i] + parts[i + 1] for i in range(0, len(parts), 2)]
    return parts[0]


def by_mode(rows, values, order):
    for k in range(ROWS):
        rows[pl.ds(k * order, order), :] = values[:, k * LANES : (k + 1) * LANES]
    return [rows[pl.ds(n, ROWS, stride=order), :] for n in range(order)]


def state_kernel(order, length, pitch, total,
                 inputs, tap_source, rate_source, end_ref, span_ref, head, gate,
                 held_inputs, taps, rates, raw, mode_rows, sems):
    groups = held_inputs.shape[0]

    def fetch(g):
        return pltpu.make_async_copy(
            inputs.at[0, pl.ds(1, 2), :, pl.ds(g * GROUP, GROUP)], held_inputs.at[g], sems.at[g]
        )

    tap_copy = pltpu.make_async_copy(tap_source, taps, sems.at[groups])
    rate_copy = pltpu.make_async_copy(rate_source.at[0], rates, sems.at[groups + 1])
    fetch(0).start()
    tap_copy.start()
    rate_copy.start()
    for g in range(1, groups):
        fetch(g).start()
    zero = jnp.zeros((ROWS, LANES), f32)

    for g in range(groups):
        at = pl.ds(g * ROWS, ROWS)
        fetch(g).wait()
        for i in range(2):
            for k in range(ROWS):
                raw[i, pl.ds(k * pitch + 8, length), :] = held_inputs[g, i, :, k * LANES : (k + 1) * LANES].astype(f32)
        if g == 0:
            tap_copy.wait()
            rate_copy.wait()

        def token(i, t):
            return raw[i, pl.ds(8 + t, ROWS, stride=pitch), :]

        weights = [[taps[TAPS * (1 + i) + a, at, :] for a in range(TAPS)] for i in range(2)]

        def features(t, before):
            after, made = [], []
            for i in range(2):
                now = token(i, t)
                one, two = before[i]
                made.append(weights[i][0] * now + weights[i][1] * one + weights[i][2] * two)
                after.append((now, one))
            return tuple(after), made

        def feature_step(pair, before):
            gates = []
            for sub in range(2):
                before, made = features(2 * pair + sub, before)
                gates.append(made[0] * made[1])
            gate[g, pair] = jnp.concatenate(gates, axis=0).astype(bf16)
            return before

        before = ((zero, zero),) * 2
        for t in range(TAPS - 1):
            before, made = features(t, before)
            for i in range(2):
                head[2 * i + t, at, :] = made[i]
        lax.fori_loop(1, length // 2, feature_step, before, unroll=9)

        steps = []
        for n, rate in enumerate(by_mode(mode_rows, rates[:, g * GROUP : (g + 1) * GROUP], order)):
            span_ref[n, at, :] = rate * (length / total)
            steps.append(jnp.exp(-(rate / total)))

        def state_step(pair, states):
            both = gate[g, pair].astype(f32)
            for sub in range(2):
                gated = both[sub * ROWS : (sub + 1) * ROWS]
                states = tuple(s * x + gated for s, x in zip(steps, states))
            return states

        states = lax.fori_loop(1, length // 2, state_step, (zero,) * order, unroll=9)
        for n in range(order):
            end_ref[n, at, :] = states[n]


def patch_kernel(order, length, rim, head, taps, ends, span, wire, edge, rows):
    tiles = ends.shape[1]
    for i in range(3):
        came = rim[0, i].astype(f32)
        for t in range(TAPS - 1):
            for k in range(tiles):
                rows[2 * i + t, pl.ds(k, 1), :] = came[t : t + 1, k * LANES : (k + 1) * LANES]
    edge[0] = rows[0]
    edge[1] = rows[1]
    made = []
    for i in range(1, 3):
        two, one = rows[2 * i], rows[2 * i + 1]
        made.append((head[2 * i - 2] + taps[TAPS * i + 1] * one + taps[TAPS * i + 2] * two,
                     head[2 * i - 1] + taps[TAPS * i + 2] * one))
    gated = []
    for t in range(2):
        gated.append((made[0][t] * made[1][t]).astype(bf16).astype(f32))
        edge[2 + t] = gated[t]
    for n in range(order):
        step = span[n] * (1.0 / length)
        first = jnp.exp(-step) * gated[0] + gated[1]
        wire[n] = (ends[n] + jnp.exp(-(length - 2) * step) * first).astype(bf16)


def mix_kernel(order, length, pitch, total, inputs, taps, gate, edge, rates, scaled, skip, lead, mix, raw, mode_rows):
    steps = [jnp.exp(-(rate / total)) for rate in by_mode(mode_rows, rates[0], order)]
    scales = by_mode(mode_rows, scaled[...], order)
    weights = [taps[a] for a in range(TAPS)]
    for k in range(ROWS):
        raw[pl.ds(k * pitch, length), :] = inputs[0, 0, :, k * LANES : (k + 1) * LANES].astype(f32)

    def lead_step(pair, before):
        for sub in range(2):
            t = 2 * pair + sub
            one, two = before
            now = raw[pl.ds(t, ROWS, stride=pitch), :]
            lead[0, t] = weights[0] * now + weights[1] * one + weights[2] * two
            before = (now, one)
        return before

    lax.fori_loop(0, length // 2, lead_step, (edge[1], edge[0]), unroll=4)

    def tokens(pair, states, both):
        for sub, gated in enumerate(both):
            states = tuple(s * x + gated for s, x in zip(steps, states))
            mix[0, 2 * pair + sub] = tree_sum([w * x for w, x in zip(scales, states)]) + skip[...] * gated
        return states

    def step(pair, states):
        both = gate[0, pair].astype(f32)
        return tokens(pair, states, (both[:ROWS], both[ROWS:]))

    states = tokens(0, (jnp.zeros((ROWS, LANES), f32),) * order, (edge[2], edge[3]))
    lax.fori_loop(1, length // 2, step, states, unroll=3)


def finish_kernel(order, length, pitch, total, first, count, *refs):
    sources, (rates, scaled, start, out_ref, parts, rows, mode_rows, sems) = refs[: 2 * count], refs[2 * count :]
    piece = length // PIECES

    def fetch(g, i, c):
        which, at = 2 * g + i, pl.ds(c * piece, piece)
        return pltpu.make_async_copy(sources[which].at[0, at], parts.at[which, at], sems.at[which, c])

    for g in range(count):
        for c in range(PIECES):
            for i in range(2):
                fetch(g, i, c).start()
    for g in range(count):
        lanes = slice((first + g) * GROUP, (first + g + 1) * GROUP)
        steps = [jnp.exp(-(rate / total)) for rate in by_mode(mode_rows, rates[0, :, lanes], order)]
        scales = by_mode(mode_rows, scaled[:, lanes], order)
        pair = (first + g) // 2 * 2 * ROWS
        states = start[:, pair : pair + 2 * ROWS, :].astype(f32)
        states = states[:, (first + g) % 2 * ROWS : ((first + g) % 2 + 1) * ROWS]

        def step(t, terms):
            terms = tuple(s * x for s, x in zip(steps, terms))
            rows[pl.ds(t, ROWS, stride=pitch), :] = parts[2 * g, t] * (parts[2 * g + 1, t] + tree_sum(list(terms)))
            return terms

        terms = tuple(scales[n] * states[n] for n in range(order))
        for c in range(PIECES):
            for i in range(2):
                fetch(g, i, c).wait()
            terms = lax.fori_loop(c * piece, (c + 1) * piece, step, terms, unroll=8)
        for k in range(ROWS):
            lanes = slice(g * GROUP + k * LANES, g * GROUP + (k + 1) * LANES)
            out_ref[0, :, lanes] = rows[pl.ds(k * pitch, length), :].astype(bf16)


def whole_kernel(order, length, pitch, total, odd, inputs, taps, gate, edge, rates, scaled, skip, start, out_ref,
                 raw, rows, mode_rows, start_rows):
    steps = [jnp.exp(-(rate / total)) for rate in by_mode(mode_rows, rates[0], order)]
    scales = by_mode(mode_rows, scaled[...], order)
    start_rows[...] = start[...].astype(f32)
    at = pl.ds(odd * ROWS, ROWS)
    weights = [taps[a] for a in range(TAPS)]
    for k in range(ROWS):
        raw[pl.ds(k * pitch, length), :] = inputs[0, 0, :, k * LANES : (k + 1) * LANES].astype(f32)

    def lead_step(pair, before):
        for sub in range(2):
            t = 2 * pair + sub
            one, two = before
            now = raw[pl.ds(t, ROWS, stride=pitch), :]
            rows[pl.ds(t, ROWS, stride=pitch), :] = weights[0] * now + weights[1] * one + weights[2] * two
            before = (now, one)
        return before

    lax.fori_loop(0, length // 2, lead_step, (edge[1], edge[0]), unroll=4)

    def tokens(pair, states, both):
        for sub, gated in enumerate(both):
            t = 2 * pair + sub
            states = tuple(s * x + gated for s, x in zip(steps, states))
            mixed = tree_sum([w * x for w, x in zip(scales, states)]) + skip[...] * gated
            raw[pl.ds(t, ROWS, stride=pitch), :] = rows[pl.ds(t, ROWS, stride=pitch), :] * mixed
        return states

    def step(pair, states):
        both = gate[0, pair].astype(f32)
        return tokens(pair, states, (both[:ROWS], both[ROWS:]))

    states = tokens(0, tuple(start_rows[n, at, :] for n in range(order)), (edge[2], edge[3]))
    lax.fori_loop(1, length // 2, step, states, unroll=3)
    for k in range(ROWS):
        out_ref[0, :, pl.ds(k * LANES, LANES)] = raw[pl.ds(k * pitch, length), :].astype(bf16)


def place_kernel(part, *rest):
    rest[-1][...] = part[...]


def scan_kernel(came, span, enter):
    keep = jnp.exp(-span[lax.axis_index("seq")])
    state = jnp.zeros(keep.shape, f32)
    for j in range(came.shape[0]):
        enter[j] = state.astype(bf16)
        state = keep * state + came[j].astype(f32)


def after(*arrays):
    return lax.optimization_barrier(arrays)


def call(body, name, groups, ops, length, in_specs, out_specs, out_shape, scratch, aliases={}):
    return pl.pallas_call(
        body,
        grid=(groups,),
        in_specs=in_specs,
        out_specs=out_specs,
        out_shape=out_shape,
        scratch_shapes=scratch,
        input_output_aliases=aliases,
        compiler_params=pltpu.CompilerParams(vmem_limit_bytes=16 << 20),
        cost_estimate=pl.CostEstimate(
            flops=ops * length * groups * GROUP, bytes_accessed=8 * length * groups * GROUP, transcendentals=0
        ),
        name=name,
    )


def shards(projected, short_filter, decay_rate, residue, skip_gain):
    length, width = projected.shape[2:]
    order = decay_rate.shape[1]
    nseq = lax.axis_size("seq")
    sections = lax.axis_size("pipe")
    total = length * nseq
    groups = width // GROUP
    tiles = width // LANES
    pitch = length + 8
    onward = [(i, i + 1) for i in range(sections - 1)]
    held = lambda x: pltpu.with_memory_space_constraint(x, pltpu.HBM)
    to_all = lambda x: lax.all_to_all(x, "seq", 0, 0, tiled=True)
    taps = short_filter.reshape(3 * TAPS, tiles, LANES)
    skip = skip_gain.reshape(tiles, LANES)
    rim = lax.ppermute(projected[:, :, length - (TAPS - 1) :, :], "seq", [(i, i + 1) for i in range(nseq - 1)])

    tokens = lambda at: pl.BlockSpec((1, length, ROWS, LANES), lambda g: (at + g, 0, 0, 0))
    pairs = lambda at: pl.BlockSpec((1, length // 2, 2 * ROWS, LANES), lambda g: (at + g, 0, 0, 0))
    stack = lambda n, at: pl.BlockSpec((n, ROWS, LANES), lambda g: (0, at + g, 0))
    rate_block = lambda at: pl.BlockSpec((1, order, GROUP), lambda g: (0, 0, at + g))
    scale_block = lambda at: pl.BlockSpec((order, GROUP), lambda g: (0, at + g))
    out_block = lambda at: pl.BlockSpec((1, length, GROUP), lambda g: (0, 0, at + g))
    anywhere = pl.BlockSpec(memory_space=pl.ANY)
    shape = lambda *dims: jax.ShapeDtypeStruct(dims, f32)
    mode_rows = pltpu.VMEM((ROWS * order, LANES), f32)
    ends, span, head, gate = pl.pallas_call(
        functools.partial(state_kernel, order, length, pitch, total),
        in_specs=[anywhere] * 3,
        out_shape=[
            shape(order, tiles, LANES), shape(order, tiles, LANES), shape(4, tiles, LANES),
            jax.ShapeDtypeStruct((groups, length // 2, 2 * ROWS, LANES), bf16),
        ],
        scratch_shapes=[
            pltpu.VMEM((groups, 2, length, GROUP), bf16),
            pltpu.VMEM((3 * TAPS, tiles, LANES), f32),
            pltpu.VMEM((order, width), f32),
            pltpu.VMEM((2, ROWS * pitch, LANES), f32),
            mode_rows,
            pltpu.SemaphoreType.DMA((groups + 2,)),
        ],
        compiler_params=pltpu.CompilerParams(vmem_limit_bytes=16 << 20),
        cost_estimate=pl.CostEstimate(flops=55 * length * width, bytes_accessed=8 * length * width, transcendentals=0),
        name="local_states",
    )(held(projected), held(taps), held(decay_rate))
    wire, edge = pl.pallas_call(
        functools.partial(patch_kernel, order, length),
        out_shape=[jax.ShapeDtypeStruct((order, tiles, LANES), bf16), shape(4, tiles, LANES)],
        scratch_shapes=[pltpu.VMEM((6, tiles, LANES), f32)],
        compiler_params=pltpu.CompilerParams(vmem_limit_bytes=8 << 20),
        name="first_tokens",
    )(rim, head, taps, ends, span)

    def local_mix(at, gated):
        return call(
            functools.partial(mix_kernel, order, length, pitch, total), "local_mix", 1, 80, length,
            [pl.BlockSpec((1, 1, length, GROUP), lambda g: (0, 0, 0, at + g)), stack(TAPS, at),
             pairs(at), stack(4, at), rate_block(at), scale_block(at),
             pl.BlockSpec((ROWS, LANES), lambda g: (at + g, 0))],
            [tokens(0), tokens(0)], [pltpu.HBM((1, length, ROWS, LANES), f32)] * 2,
            [pltpu.VMEM((ROWS * pitch, LANES), f32), mode_rows],
        )(held(projected), held(taps), gated, edge, held(decay_rate), scaled, held(skip))

    wire, gate, residue = after(wire, gate, residue)
    scaled = residue[0] * jnp.sqrt(-jnp.expm1(-2.0 * (decay_rate[0] / total)))
    came = to_all(wire)
    mixes = [local_mix(0, gate)]
    came, mixes, gate = after(came, mixes, gate)
    enter = pl.pallas_call(
        scan_kernel,
        out_shape=jax.ShapeDtypeStruct(came.shape, bf16),
        compiler_params=pltpu.CompilerParams(vmem_limit_bytes=4 << 20),
        name="scan_chunks",
    )(came, span)
    enter, gate = after(enter, gate)
    start = to_all(enter)
    mixes.append(local_mix(1, gate))
    start, mixes, gate = after(start, mixes, gate)
    in_vmem = pl.BlockSpec(memory_space=pltpu.VMEM)
    share = jax.ShapeDtypeStruct((1, length, GROUP), bf16)
    handed = None
    for at in range(groups):
        if at < EARLY:
            output = pl.pallas_call(
                functools.partial(finish_kernel, order, length, pitch, total, at, 1),
                in_specs=[anywhere] * 2 + [in_vmem] * 3,
                out_specs=in_vmem,
                out_shape=share,
                scratch_shapes=[
                    pltpu.VMEM((2, length, ROWS, LANES), f32),
                    pltpu.VMEM((ROWS * pitch, LANES), f32),
                    mode_rows,
                    pltpu.SemaphoreType.DMA((2, PIECES)),
                ],
                compiler_params=pltpu.CompilerParams(vmem_limit_bytes=16 << 20),
                cost_estimate=pl.CostEstimate(
                    flops=40 * length * GROUP, bytes_accessed=8 * length * GROUP, transcendentals=0
                ),
                name="finished",
            )(*map(held, mixes[at]), decay_rate, scaled, start)
        else:
            output = call(
                functools.partial(whole_kernel, order, length, pitch, total, at % 2), "mixed_output", 1, 90, length,
                [pl.BlockSpec((1, 1, length, GROUP), lambda g, at=at: (0, 0, 0, at)), stack(TAPS, at),
                 pairs(at), stack(4, at), rate_block(at), scale_block(at),
                 pl.BlockSpec((ROWS, LANES), lambda g, at=at: (at, 0)),
                 pl.BlockSpec((order, 2 * ROWS, LANES), lambda g, at=at: (0, at // 2, 0))],
                out_block(0), share,
                [pltpu.VMEM((ROWS * pitch, LANES), f32)] * 2
                + [mode_rows, pltpu.VMEM((order, 2 * ROWS, LANES), f32)],
            )(held(projected), held(taps), gate, edge, held(decay_rate), scaled, held(skip), start)
        came = lax.ppermute(output, "pipe", onward)
        given = [came] if handed is None else [came, handed]
        handed = call(
            place_kernel, "placed", 1, PLACE_OPS, length, [out_block(0)] + [anywhere] * (len(given) - 1),
            out_block(at), jax.ShapeDtypeStruct((1, length, width), bf16), [], {1: 0} if len(given) > 1 else {},
        )(*given)
    return handed


def solution(mesh):
    in_specs = (
        P("pipe", None, "seq", None),
        P("pipe", None, None, None),
        P("pipe", None, None),
        P("pipe", None, None),
        P("pipe", None),
    )
    out_specs = P("pipe", "seq", None)
    return jax.shard_map(shards, mesh=mesh, in_specs=in_specs, out_specs=out_specs, check_vma=False)
```

```python
import functools

import jax
import jax.numpy as jnp
from jax import lax
from jax.experimental import pallas as pl
from jax.experimental.pallas import tpu as pltpu
from jax.sharding import PartitionSpec as P

TAPS = 3
LANES = 128
ROWS = 8
GROUP = ROWS * LANES
EARLY = 2
FIRST_OPS = 25600
PLACE_OPS = 10000
UNPACK = 0
PIECES = 4
f32 = jnp.float32
bf16 = jnp.bfloat16


def tree_sum(parts):
    while len(parts) > 1:
        parts = [parts[i] + parts[i + 1] for i in range(0, len(parts), 2)]
    return parts[0]


def by_mode(rows, values, order):
    for k in range(ROWS):
        rows[pl.ds(k * order, order), :] = values[:, k * LANES : (k + 1) * LANES]
    return [rows[pl.ds(n, ROWS, stride=order), :] for n in range(order)]


def state_kernel(order, length, pitch, total,
                 inputs, tap_source, rate_source, end_ref, span_ref, head, gate,
                 held_inputs, taps, rates, raw, mode_rows, sems):
    groups = held_inputs.shape[0]

    def fetch(g):
        return pltpu.make_async_copy(
            inputs.at[0, pl.ds(1, 2), :, pl.ds(g * GROUP, GROUP)], held_inputs.at[g], sems.at[g]
        )

    tap_copy = pltpu.make_async_copy(tap_source, taps, sems.at[groups])
    rate_copy = pltpu.make_async_copy(rate_source.at[0], rates, sems.at[groups + 1])
    fetch(0).start()
    tap_copy.start()
    rate_copy.start()
    for g in range(1, groups):
        fetch(g).start()
    zero = jnp.zeros((ROWS, LANES), f32)

    for g in range(groups):
        at = pl.ds(g * ROWS, ROWS)
        fetch(g).wait()
        for i in range(2):
            for k in range(ROWS):
                raw[i, pl.ds(k * pitch + 8, length), :] = held_inputs[g, i, :, k * LANES : (k + 1) * LANES].astype(f32)
        if g == 0:
            tap_copy.wait()
            rate_copy.wait()

        def token(i, t):
            return raw[i, pl.ds(8 + t, ROWS, stride=pitch), :]

        weights = [[taps[TAPS * (1 + i) + a, at, :] for a in range(TAPS)] for i in range(2)]

        def features(t, before):
            after, made = [], []
            for i in range(2):
                now = token(i, t)
                one, two = before[i]
                made.append(weights[i][0] * now + weights[i][1] * one + weights[i][2] * two)
                after.append((now, one))
            return tuple(after), made

        def feature_step(pair, before):
            gates = []
            for sub in range(2):
                before, made = features(2 * pair + sub, before)
                gates.append(made[0] * made[1])
            gate[g, pair] = jnp.concatenate(gates, axis=0).astype(bf16)
            return before

        before = ((zero, zero),) * 2
        for t in range(TAPS - 1):
            before, made = features(t, before)
            for i in range(2):
                head[2 * i + t, at, :] = made[i]
        lax.fori_loop(1, length // 2, feature_step, before, unroll=9)

        steps = []
        for n, rate in enumerate(by_mode(mode_rows, rates[:, g * GROUP : (g + 1) * GROUP], order)):
            span_ref[n, at, :] = rate * (length / total)
            steps.append(jnp.exp(-(rate / total)))

        def state_step(pair, states):
            both = gate[g, pair].astype(f32)
            for sub in range(2):
                gated = both[sub * ROWS : (sub + 1) * ROWS]
                states = tuple(s * x + gated for s, x in zip(steps, states))
            return states

        states = lax.fori_loop(1, length // 2, state_step, (zero,) * order, unroll=9)
        for n in range(order):
            end_ref[n, at, :] = states[n]


def patch_kernel(order, length, rim, head, taps, ends, span, wire, edge, rows):
    tiles = ends.shape[1]
    for i in range(3):
        came = rim[0, i].astype(f32)
        for t in range(TAPS - 1):
            for k in range(tiles):
                rows[2 * i + t, pl.ds(k, 1), :] = came[t : t + 1, k * LANES : (k + 1) * LANES]
    edge[0] = rows[0]
    edge[1] = rows[1]
    made = []
    for i in range(1, 3):
        two, one = rows[2 * i], rows[2 * i + 1]
        made.append((head[2 * i - 2] + taps[TAPS * i + 1] * one + taps[TAPS * i + 2] * two,
                     head[2 * i - 1] + taps[TAPS * i + 2] * one))
    gated = []
    for t in range(2):
        gated.append((made[0][t] * made[1][t]).astype(bf16).astype(f32))
        edge[2 + t] = gated[t]
    for n in range(order):
        step = span[n] * (1.0 / length)
        first = jnp.exp(-step) * gated[0] + gated[1]
        wire[n] = (ends[n] + jnp.exp(-(length - 2) * step) * first).astype(bf16)


def mix_kernel(order, length, pitch, total, inputs, taps, gate, edge, rates, scaled, skip, lead, mix, raw, mode_rows):
    steps = [jnp.exp(-(rate / total)) for rate in by_mode(mode_rows, rates[0], order)]
    scales = by_mode(mode_rows, scaled[...], order)
    weights = [taps[a] for a in range(TAPS)]
    for k in range(ROWS):
        raw[pl.ds(k * pitch, length), :] = inputs[0, 0, :, k * LANES : (k + 1) * LANES].astype(f32)

    def lead_step(pair, before):
        for sub in range(2):
            t = 2 * pair + sub
            one, two = before
            now = raw[pl.ds(t, ROWS, stride=pitch), :]
            lead[0, t] = weights[0] * now + weights[1] * one + weights[2] * two
            before = (now, one)
        return before

    lax.fori_loop(0, length // 2, lead_step, (edge[1], edge[0]), unroll=4)

    def tokens(pair, states, both):
        for sub, gated in enumerate(both):
            states = tuple(s * x + gated for s, x in zip(steps, states))
            mix[0, 2 * pair + sub] = tree_sum([w * x for w, x in zip(scales, states)]) + skip[...] * gated
        return states

    def step(pair, states):
        both = gate[0, pair].astype(f32)
        return tokens(pair, states, (both[:ROWS], both[ROWS:]))

    states = tokens(0, (jnp.zeros((ROWS, LANES), f32),) * order, (edge[2], edge[3]))
    lax.fori_loop(1, length // 2, step, states, unroll=3)


def pack_kernel(order, length, pitch, total, inputs, taps, gate, edge, rates, scaled, skip, packed, raw, mode_rows):
    rate_list = by_mode(mode_rows, rates[0], order)
    tiles = []
    for rate in rate_list:
        for _ in range(3):
            term = rate.astype(bf16).astype(f32)
            tiles.append(term)
            rate = rate - term
    for m in range(0, len(tiles), 2):
        packed[0, length + m // 2] = jnp.concatenate(tiles[m : m + 2], axis=0).astype(bf16)
    steps = [jnp.exp(-(rate / total)) for rate in rate_list]
    scales = by_mode(mode_rows, scaled[...], order)
    weights = [taps[a] for a in range(TAPS)]
    for k in range(ROWS):
        raw[pl.ds(k * pitch, length), :] = inputs[0, 0, :, k * LANES : (k + 1) * LANES].astype(f32)

    def lead_step(pair, before):
        leads = []
        for sub in range(2):
            one, two = before
            now = raw[pl.ds(2 * pair + sub, ROWS, stride=pitch), :]
            leads.append(weights[0] * now + weights[1] * one + weights[2] * two)
            before = (now, one)
        packed[0, pair] = jnp.concatenate(leads, axis=0).astype(bf16)
        return before

    lax.fori_loop(0, length // 2, lead_step, (edge[1], edge[0]), unroll=4)

    def tokens(pair, states, both):
        mixes = []
        for gated in both:
            states = tuple(s * x + gated for s, x in zip(steps, states))
            mixes.append(tree_sum([w * x for w, x in zip(scales, states)]) + skip[...] * gated)
        packed[0, length // 2 + pair] = jnp.concatenate(mixes, axis=0).astype(bf16)
        return states

    def step(pair, states):
        both = gate[0, pair].astype(f32)
        return tokens(pair, states, (both[:ROWS], both[ROWS:]))

    states = tokens(0, (jnp.zeros((ROWS, LANES), f32),) * order, (edge[2], edge[3]))
    lax.fori_loop(1, length // 2, step, states, unroll=3)


def unpack_kernel(order, length, pitch, total, packed, start, *rest):
    out_ref, rows = rest[-2:]
    tiles = []
    for m in range(0, 3 * order, 2):
        both = packed[0, length + m // 2].astype(f32)
        tiles += [both[:ROWS], both[ROWS:]]
    steps = [jnp.exp(-((tiles[3 * n] + tiles[3 * n + 1] + tiles[3 * n + 2]) / total)) for n in range(order)]

    def step(pair, terms):
        lead, mix = packed[0, pair].astype(f32), packed[0, length // 2 + pair].astype(f32)
        for sub in range(2):
            part = slice(sub * ROWS, (sub + 1) * ROWS)
            terms = tuple(s * x for s, x in zip(steps, terms))
            rows[pl.ds(2 * pair + sub, ROWS, stride=pitch), :] = lead[part] * (mix[part] + tree_sum(list(terms)))
        return terms

    lax.fori_loop(0, length // 2, step, tuple(start[n] for n in range(order)), unroll=4)
    for k in range(ROWS):
        out_ref[0, :, pl.ds(k * LANES, LANES)] = rows[pl.ds(k * pitch, length), :].astype(bf16)


def finish_kernel(order, length, pitch, total, first, count, *refs):
    sources, (rates, scaled, start, out_ref, parts, rows, mode_rows, sems) = refs[: 2 * count], refs[2 * count :]
    piece = length // PIECES

    def fetch(g, i, c):
        which, at = 2 * g + i, pl.ds(c * piece, piece)
        return pltpu.make_async_copy(sources[which].at[first, at], parts.at[which, at], sems.at[which, c])

    for g in range(count):
        for c in range(PIECES):
            for i in range(2):
                fetch(g, i, c).start()
    for g in range(count):
        lanes = slice((first + g) * GROUP, (first + g + 1) * GROUP)
        steps = [jnp.exp(-(rate / total)) for rate in by_mode(mode_rows, rates[0, :, lanes], order)]
        scales = by_mode(mode_rows, scaled[:, lanes], order)
        pair = (first + g) // 2 * 2 * ROWS
        states = start[:, pair : pair + 2 * ROWS, :].astype(f32)
        states = states[:, (first + g) % 2 * ROWS : ((first + g) % 2 + 1) * ROWS]

        def step(t, terms):
            terms = tuple(s * x for s, x in zip(steps, terms))
            rows[pl.ds(t, ROWS, stride=pitch), :] = parts[2 * g, t] * (parts[2 * g + 1, t] + tree_sum(list(terms)))
            return terms

        terms = tuple(scales[n] * states[n] for n in range(order))
        for c in range(PIECES):
            for i in range(2):
                fetch(g, i, c).wait()
            terms = lax.fori_loop(c * piece, (c + 1) * piece, step, terms, unroll=8)
        for k in range(ROWS):
            lanes = slice(g * GROUP + k * LANES, g * GROUP + (k + 1) * LANES)
            out_ref[0, :, lanes] = rows[pl.ds(k * pitch, length), :].astype(bf16)


def whole_kernel(order, length, pitch, total, odd, inputs, taps, gate, edge, rates, scaled, skip, start, out_ref,
                 raw, rows, mode_rows, start_rows):
    steps = [jnp.exp(-(rate / total)) for rate in by_mode(mode_rows, rates[0], order)]
    scales = by_mode(mode_rows, scaled[...], order)
    start_rows[...] = start[...].astype(f32)
    at = pl.ds(odd * ROWS, ROWS)
    weights = [taps[a] for a in range(TAPS)]
    for k in range(ROWS):
        raw[pl.ds(k * pitch, length), :] = inputs[0, 0, :, k * LANES : (k + 1) * LANES].astype(f32)

    def lead_step(pair, before):
        for sub in range(2):
            t = 2 * pair + sub
            one, two = before
            now = raw[pl.ds(t, ROWS, stride=pitch), :]
            rows[pl.ds(t, ROWS, stride=pitch), :] = weights[0] * now + weights[1] * one + weights[2] * two
            before = (now, one)
        return before

    lax.fori_loop(0, length // 2, lead_step, (edge[1], edge[0]), unroll=4)

    def tokens(pair, states, both):
        for sub, gated in enumerate(both):
            t = 2 * pair + sub
            states = tuple(s * x + gated for s, x in zip(steps, states))
            mixed = tree_sum([w * x for w, x in zip(scales, states)]) + skip[...] * gated
            raw[pl.ds(t, ROWS, stride=pitch), :] = rows[pl.ds(t, ROWS, stride=pitch), :] * mixed
        return states

    def step(pair, states):
        both = gate[0, pair].astype(f32)
        return tokens(pair, states, (both[:ROWS], both[ROWS:]))

    states = tokens(0, tuple(start_rows[n, at, :] for n in range(order)), (edge[2], edge[3]))
    lax.fori_loop(1, length // 2, step, states, unroll=3)
    for k in range(ROWS):
        out_ref[0, :, pl.ds(k * LANES, LANES)] = raw[pl.ds(k * pitch, length), :].astype(bf16)


def place_kernel(part, *rest):
    rest[-1][...] = part[...]


def scan_kernel(came, span, enter):
    keep = jnp.exp(-span[lax.axis_index("seq")])
    state = jnp.zeros(keep.shape, f32)
    for j in range(came.shape[0]):
        enter[j] = state.astype(bf16)
        state = keep * state + came[j].astype(f32)


def after(*arrays):
    return lax.optimization_barrier(arrays)


def call(body, name, groups, ops, length, in_specs, out_specs, out_shape, scratch, aliases={}):
    return pl.pallas_call(
        body,
        grid=(groups,),
        in_specs=in_specs,
        out_specs=out_specs,
        out_shape=out_shape,
        scratch_shapes=scratch,
        input_output_aliases=aliases,
        compiler_params=pltpu.CompilerParams(vmem_limit_bytes=16 << 20),
        cost_estimate=pl.CostEstimate(
            flops=ops * length * groups * GROUP, bytes_accessed=8 * length * groups * GROUP, transcendentals=0
        ),
        name=name,
    )


def shards(projected, short_filter, decay_rate, residue, skip_gain):
    length, width = projected.shape[2:]
    order = decay_rate.shape[1]
    nseq = lax.axis_size("seq")
    sections = lax.axis_size("pipe")
    total = length * nseq
    groups = width // GROUP
    tiles = width // LANES
    pitch = length + 8
    onward = [(i, i + 1) for i in range(sections - 1)]
    held = lambda x: pltpu.with_memory_space_constraint(x, pltpu.HBM)
    to_all = lambda x: lax.all_to_all(x, "seq", 0, 0, tiled=True)
    taps = short_filter.reshape(3 * TAPS, tiles, LANES)
    skip = skip_gain.reshape(tiles, LANES)
    rim = lax.ppermute(projected[:, :, length - (TAPS - 1) :, :], "seq", [(i, i + 1) for i in range(nseq - 1)])

    tokens = lambda at: pl.BlockSpec((1, length, ROWS, LANES), lambda g: (at + g, 0, 0, 0))
    pairs = lambda at: pl.BlockSpec((1, length // 2, 2 * ROWS, LANES), lambda g: (at + g, 0, 0, 0))
    stack = lambda n, at: pl.BlockSpec((n, ROWS, LANES), lambda g: (0, at + g, 0))
    rate_block = lambda at: pl.BlockSpec((1, order, GROUP), lambda g: (0, 0, at + g))
    scale_block = lambda at: pl.BlockSpec((order, GROUP), lambda g: (0, at + g))
    out_block = lambda at: pl.BlockSpec((1, length, GROUP), lambda g: (0, 0, at + g))
    anywhere = pl.BlockSpec(memory_space=pl.ANY)
    shape = lambda *dims: jax.ShapeDtypeStruct(dims, f32)
    mode_rows = pltpu.VMEM((ROWS * order, LANES), f32)
    ends, span, head, gate = pl.pallas_call(
        functools.partial(state_kernel, order, length, pitch, total),
        in_specs=[anywhere] * 3,
        out_shape=[
            shape(order, tiles, LANES), shape(order, tiles, LANES), shape(4, tiles, LANES),
            jax.ShapeDtypeStruct((groups, length // 2, 2 * ROWS, LANES), bf16),
        ],
        scratch_shapes=[
            pltpu.VMEM((groups, 2, length, GROUP), bf16),
            pltpu.VMEM((3 * TAPS, tiles, LANES), f32),
            pltpu.VMEM((order, width), f32),
            pltpu.VMEM((2, ROWS * pitch, LANES), f32),
            mode_rows,
            pltpu.SemaphoreType.DMA((groups + 2,)),
        ],
        compiler_params=pltpu.CompilerParams(vmem_limit_bytes=16 << 20),
        cost_estimate=pl.CostEstimate(flops=55 * length * width, bytes_accessed=8 * length * width, transcendentals=0),
        name="local_states",
    )(held(projected), held(taps), held(decay_rate))
    wire, edge = pl.pallas_call(
        functools.partial(patch_kernel, order, length),
        out_shape=[jax.ShapeDtypeStruct((order, tiles, LANES), bf16), shape(4, tiles, LANES)],
        scratch_shapes=[pltpu.VMEM((6, tiles, LANES), f32)],
        compiler_params=pltpu.CompilerParams(vmem_limit_bytes=8 << 20),
        name="first_tokens",
    )(rim, head, taps, ends, span)

    def local_mix(at, gated):
        return call(
            functools.partial(mix_kernel, order, length, pitch, total), "local_mix", EARLY, 80, length,
            [pl.BlockSpec((1, 1, length, GROUP), lambda g: (0, 0, 0, at + g)), stack(TAPS, at),
             pairs(at), stack(4, at), rate_block(at), scale_block(at),
             pl.BlockSpec((ROWS, LANES), lambda g: (at + g, 0))],
            [tokens(0), tokens(0)], [pltpu.HBM((EARLY, length, ROWS, LANES), f32)] * 2,
            [pltpu.VMEM((ROWS * pitch, LANES), f32), mode_rows],
        )(held(projected), held(taps), gated, edge, held(decay_rate), scaled, held(skip))

    def packed_group(at, gated):
        return call(
            functools.partial(pack_kernel, order, length, pitch, total), "packed", 1, 80, length,
            [pl.BlockSpec((1, 1, length, GROUP), lambda g: (0, 0, 0, at)), stack(TAPS, at),
             pairs(at), stack(4, at), rate_block(at), scale_block(at),
             pl.BlockSpec((ROWS, LANES), lambda g: (at, 0))],
            pl.BlockSpec((1, packed_rows, 2 * ROWS, LANES), lambda g: (0, 0, 0, 0)),
            pltpu.HBM((1, packed_rows, 2 * ROWS, LANES), bf16),
            [pltpu.VMEM((ROWS * pitch, LANES), f32), mode_rows],
        )(held(projected), held(taps), gated, edge, held(decay_rate), scaled, held(skip))

    last = groups - 1
    packed_rows = length + 3 * order // 2
    wire, gate, residue = after(wire, gate, residue)
    scaled = residue[0] * jnp.sqrt(-jnp.expm1(-2.0 * (decay_rate[0] / total)))
    came = to_all(wire)
    packed = packed_group(last, gate)
    packed_before = lax.ppermute(packed, "pipe", onward)
    came, packed, gate, scaled = after(came, packed, gate, scaled)
    enter = pl.pallas_call(
        scan_kernel,
        out_shape=jax.ShapeDtypeStruct(came.shape, bf16),
        compiler_params=pltpu.CompilerParams(vmem_limit_bytes=4 << 20),
        name="scan_chunks",
    )(came, span)
    enter, gate = after(enter, gate)
    start = to_all(enter)
    mixes = local_mix(0, gate)
    start, mixes, gate = after(start, mixes, gate)
    scale_tile = scaled[:, last * GROUP :].reshape(order, ROWS, LANES)
    sent = (start[:, last * ROWS :].astype(f32) * scale_tile).astype(bf16)
    start_before = lax.ppermute(sent, "pipe", onward).astype(f32)
    in_vmem = pl.BlockSpec(memory_space=pltpu.VMEM)
    share = jax.ShapeDtypeStruct((1, length, GROUP), bf16)
    handed = None
    for at in range(last):
        if at < EARLY:
            output = pl.pallas_call(
                functools.partial(finish_kernel, order, length, pitch, total, at, 1),
                in_specs=[anywhere] * 2 + [in_vmem] * 3,
                out_specs=in_vmem,
                out_shape=share,
                scratch_shapes=[
                    pltpu.VMEM((2, length, ROWS, LANES), f32),
                    pltpu.VMEM((ROWS * pitch, LANES), f32),
                    mode_rows,
                    pltpu.SemaphoreType.DMA((2, PIECES)),
                ],
                compiler_params=pltpu.CompilerParams(vmem_limit_bytes=16 << 20),
                cost_estimate=pl.CostEstimate(
                    flops=(40 if at else FIRST_OPS) * length * GROUP, bytes_accessed=8 * length * GROUP, transcendentals=0
                ),
                name="finished",
            )(*map(held, mixes), decay_rate, scaled, start)
        else:
            output = call(
                functools.partial(whole_kernel, order, length, pitch, total, at % 2), "mixed_output", 1, 90, length,
                [pl.BlockSpec((1, 1, length, GROUP), lambda g, at=at: (0, 0, 0, at)), stack(TAPS, at),
                 pairs(at), stack(4, at), rate_block(at), scale_block(at),
                 pl.BlockSpec((ROWS, LANES), lambda g, at=at: (at, 0)),
                 pl.BlockSpec((order, 2 * ROWS, LANES), lambda g, at=at: (0, at // 2, 0))],
                out_block(0), share,
                [pltpu.VMEM((ROWS * pitch, LANES), f32)] * 2
                + [mode_rows, pltpu.VMEM((order, 2 * ROWS, LANES), f32)],
            )(held(projected), held(taps), gate, edge, held(decay_rate), scaled, held(skip), start)
        if at == 0:
            output, packed_before = after(output, packed_before)
        came = lax.ppermute(output, "pipe", onward)
        given = [came] if handed is None else [came, handed]
        handed = call(
            place_kernel, "placed", 1, PLACE_OPS, length, [out_block(0)] + [anywhere] * (len(given) - 1),
            out_block(at), jax.ShapeDtypeStruct((1, length, width), bf16), [], {1: 0} if len(given) > 1 else {},
        )(*given)
        if at == UNPACK:
            handed = call(
                functools.partial(unpack_kernel, order, length, pitch, total), "finished_ahead", 1, PLACE_OPS, length,
                [pl.BlockSpec((1, packed_rows, 2 * ROWS, LANES), lambda g: (0, 0, 0, 0)), stack(order, 0), anywhere],
                out_block(last), jax.ShapeDtypeStruct((1, length, width), bf16),
                [pltpu.VMEM((ROWS * pitch, LANES), f32)], {2: 0},
            )(packed_before, start_before, handed)
    return handed


def solution(mesh):
    in_specs = (
        P("pipe", None, "seq", None),
        P("pipe", None, None, None),
        P("pipe", None, None),
        P("pipe", None, None),
        P("pipe", None),
    )
    out_specs = P("pipe", "seq", None)
    return jax.shard_map(shards, mesh=mesh, in_specs=in_specs, out_specs=out_specs, check_vma=False)
```

```python
import functools

import jax
import jax.numpy as jnp
from jax import lax
from jax.experimental import pallas as pl
from jax.experimental.pallas import tpu as pltpu
from jax.sharding import PartitionSpec as P

TAPS = 3
LANES = 128
ROWS = 8
GROUP = ROWS * LANES
EARLY = 2
FIRST_OPS = 25600
PLACE_OPS = 10000
UNPACK = 1
PIECES = 4
f32 = jnp.float32
bf16 = jnp.bfloat16


def tree_sum(parts):
    while len(parts) > 1:
        parts = [parts[i] + parts[i + 1] for i in range(0, len(parts), 2)]
    return parts[0]


def by_mode(rows, values, order):
    for k in range(ROWS):
        rows[pl.ds(k * order, order), :] = values[:, k * LANES : (k + 1) * LANES]
    return [rows[pl.ds(n, ROWS, stride=order), :] for n in range(order)]


def state_kernel(order, length, pitch, total,
                 inputs, tap_source, rate_source, end_ref, span_ref, head, gate,
                 held_inputs, taps, rates, raw, mode_rows, sems):
    groups = held_inputs.shape[0]

    def fetch(g):
        return pltpu.make_async_copy(
            inputs.at[0, pl.ds(1, 2), :, pl.ds(g * GROUP, GROUP)], held_inputs.at[g], sems.at[g]
        )

    tap_copy = pltpu.make_async_copy(tap_source, taps, sems.at[groups])
    rate_copy = pltpu.make_async_copy(rate_source.at[0], rates, sems.at[groups + 1])
    fetch(0).start()
    tap_copy.start()
    rate_copy.start()
    for g in range(1, groups):
        fetch(g).start()
    zero = jnp.zeros((ROWS, LANES), f32)

    for g in range(groups):
        at = pl.ds(g * ROWS, ROWS)
        fetch(g).wait()
        for i in range(2):
            for k in range(ROWS):
                raw[i, pl.ds(k * pitch + 8, length), :] = held_inputs[g, i, :, k * LANES : (k + 1) * LANES].astype(f32)
        if g == 0:
            tap_copy.wait()
            rate_copy.wait()

        def token(i, t):
            return raw[i, pl.ds(8 + t, ROWS, stride=pitch), :]

        weights = [[taps[TAPS * (1 + i) + a, at, :] for a in range(TAPS)] for i in range(2)]

        def features(t, before):
            after, made = [], []
            for i in range(2):
                now = token(i, t)
                one, two = before[i]
                made.append(weights[i][0] * now + weights[i][1] * one + weights[i][2] * two)
                after.append((now, one))
            return tuple(after), made

        def feature_step(pair, before):
            gates = []
            for sub in range(2):
                before, made = features(2 * pair + sub, before)
                gates.append(made[0] * made[1])
            gate[g, pair] = jnp.concatenate(gates, axis=0).astype(bf16)
            return before

        before = ((zero, zero),) * 2
        for t in range(TAPS - 1):
            before, made = features(t, before)
            for i in range(2):
                head[2 * i + t, at, :] = made[i]
        lax.fori_loop(1, length // 2, feature_step, before, unroll=9)

        steps = []
        for n, rate in enumerate(by_mode(mode_rows, rates[:, g * GROUP : (g + 1) * GROUP], order)):
            span_ref[n, at, :] = rate * (length / total)
            steps.append(jnp.exp(-(rate / total)))

        def state_step(pair, states):
            both = gate[g, pair].astype(f32)
            for sub in range(2):
                gated = both[sub * ROWS : (sub + 1) * ROWS]
                states = tuple(s * x + gated for s, x in zip(steps, states))
            return states

        states = lax.fori_loop(1, length // 2, state_step, (zero,) * order, unroll=9)
        for n in range(order):
            end_ref[n, at, :] = states[n]


def patch_kernel(order, length, rim, head, taps, ends, span, wire, edge, rows):
    tiles = ends.shape[1]
    for i in range(3):
        came = rim[0, i].astype(f32)
        for t in range(TAPS - 1):
            for k in range(tiles):
                rows[2 * i + t, pl.ds(k, 1), :] = came[t : t + 1, k * LANES : (k + 1) * LANES]
    edge[0] = rows[0]
    edge[1] = rows[1]
    made = []
    for i in range(1, 3):
        two, one = rows[2 * i], rows[2 * i + 1]
        made.append((head[2 * i - 2] + taps[TAPS * i + 1] * one + taps[TAPS * i + 2] * two,
                     head[2 * i - 1] + taps[TAPS * i + 2] * one))
    gated = []
    for t in range(2):
        gated.append((made[0][t] * made[1][t]).astype(bf16).astype(f32))
        edge[2 + t] = gated[t]
    for n in range(order):
        step = span[n] * (1.0 / length)
        first = jnp.exp(-step) * gated[0] + gated[1]
        wire[n] = (ends[n] + jnp.exp(-(length - 2) * step) * first).astype(bf16)


def mix_kernel(order, length, pitch, total, inputs, taps, gate, edge, rates, scaled, skip, lead, mix, raw, mode_rows):
    steps = [jnp.exp(-(rate / total)) for rate in by_mode(mode_rows, rates[0], order)]
    scales = by_mode(mode_rows, scaled[...], order)
    weights = [taps[a] for a in range(TAPS)]
    for k in range(ROWS):
        raw[pl.ds(k * pitch, length), :] = inputs[0, 0, :, k * LANES : (k + 1) * LANES].astype(f32)

    def lead_step(pair, before):
        for sub in range(2):
            t = 2 * pair + sub
            one, two = before
            now = raw[pl.ds(t, ROWS, stride=pitch), :]
            lead[0, t] = weights[0] * now + weights[1] * one + weights[2] * two
            before = (now, one)
        return before

    lax.fori_loop(0, length // 2, lead_step, (edge[1], edge[0]), unroll=4)

    def tokens(pair, states, both):
        for sub, gated in enumerate(both):
            states = tuple(s * x + gated for s, x in zip(steps, states))
            mix[0, 2 * pair + sub] = tree_sum([w * x for w, x in zip(scales, states)]) + skip[...] * gated
        return states

    def step(pair, states):
        both = gate[0, pair].astype(f32)
        return tokens(pair, states, (both[:ROWS], both[ROWS:]))

    states = tokens(0, (jnp.zeros((ROWS, LANES), f32),) * order, (edge[2], edge[3]))
    lax.fori_loop(1, length // 2, step, states, unroll=3)


def pack_kernel(order, length, pitch, total, inputs, taps, gate, edge, rates, scaled, skip, packed, raw, mode_rows):
    rate_list = by_mode(mode_rows, rates[0], order)
    tiles = []
    for rate in rate_list:
        for _ in range(3):
            term = rate.astype(bf16).astype(f32)
            tiles.append(term)
            rate = rate - term
    for m in range(0, len(tiles), 2):
        packed[0, length + m // 2] = jnp.concatenate(tiles[m : m + 2], axis=0).astype(bf16)
    steps = [jnp.exp(-(rate / total)) for rate in rate_list]
    scales = by_mode(mode_rows, scaled[...], order)
    weights = [taps[a] for a in range(TAPS)]
    for k in range(ROWS):
        raw[pl.ds(k * pitch, length), :] = inputs[0, 0, :, k * LANES : (k + 1) * LANES].astype(f32)

    def lead_step(pair, before):
        leads = []
        for sub in range(2):
            one, two = before
            now = raw[pl.ds(2 * pair + sub, ROWS, stride=pitch), :]
            leads.append(weights[0] * now + weights[1] * one + weights[2] * two)
            before = (now, one)
        packed[0, pair] = jnp.concatenate(leads, axis=0).astype(bf16)
        return before

    lax.fori_loop(0, length // 2, lead_step, (edge[1], edge[0]), unroll=4)

    def tokens(pair, states, both):
        mixes = []
        for gated in both:
            states = tuple(s * x + gated for s, x in zip(steps, states))
            mixes.append(tree_sum([w * x for w, x in zip(scales, states)]) + skip[...] * gated)
        packed[0, length // 2 + pair] = jnp.concatenate(mixes, axis=0).astype(bf16)
        return states

    def step(pair, states):
        both = gate[0, pair].astype(f32)
        return tokens(pair, states, (both[:ROWS], both[ROWS:]))

    states = tokens(0, (jnp.zeros((ROWS, LANES), f32),) * order, (edge[2], edge[3]))
    lax.fori_loop(1, length // 2, step, states, unroll=3)


def unpack_kernel(order, length, pitch, total, packed, start, *rest):
    out_ref, rows = rest[-2:]
    tiles = []
    for m in range(0, 3 * order, 2):
        both = packed[0, length + m // 2].astype(f32)
        tiles += [both[:ROWS], both[ROWS:]]
    steps = [jnp.exp(-((tiles[3 * n] + tiles[3 * n + 1] + tiles[3 * n + 2]) / total)) for n in range(order)]

    def step(pair, terms):
        lead, mix = packed[0, pair].astype(f32), packed[0, length // 2 + pair].astype(f32)
        for sub in range(2):
            part = slice(sub * ROWS, (sub + 1) * ROWS)
            terms = tuple(s * x for s, x in zip(steps, terms))
            rows[pl.ds(2 * pair + sub, ROWS, stride=pitch), :] = lead[part] * (mix[part] + tree_sum(list(terms)))
        return terms

    lax.fori_loop(0, length // 2, step, tuple(start[n] for n in range(order)), unroll=4)
    for k in range(ROWS):
        out_ref[0, :, pl.ds(k * LANES, LANES)] = rows[pl.ds(k * pitch, length), :].astype(bf16)


def finish_kernel(order, length, pitch, total, first, count, *refs):
    sources, (rates, scaled, start, out_ref, parts, rows, mode_rows, sems) = refs[: 2 * count], refs[2 * count :]
    piece = length // PIECES

    def fetch(g, i, c):
        which, at = 2 * g + i, pl.ds(c * piece, piece)
        return pltpu.make_async_copy(sources[which].at[first, at], parts.at[which, at], sems.at[which, c])

    for g in range(count):
        for c in range(PIECES):
            for i in range(2):
                fetch(g, i, c).start()
    for g in range(count):
        lanes = slice((first + g) * GROUP, (first + g + 1) * GROUP)
        steps = [jnp.exp(-(rate / total)) for rate in by_mode(mode_rows, rates[0, :, lanes], order)]
        scales = by_mode(mode_rows, scaled[:, lanes], order)
        pair = (first + g) // 2 * 2 * ROWS
        states = start[:, pair : pair + 2 * ROWS, :].astype(f32)
        states = states[:, (first + g) % 2 * ROWS : ((first + g) % 2 + 1) * ROWS]

        def step(t, terms):
            terms = tuple(s * x for s, x in zip(steps, terms))
            rows[pl.ds(t, ROWS, stride=pitch), :] = parts[2 * g, t] * (parts[2 * g + 1, t] + tree_sum(list(terms)))
            return terms

        terms = tuple(scales[n] * states[n] for n in range(order))
        for c in range(PIECES):
            for i in range(2):
                fetch(g, i, c).wait()
            terms = lax.fori_loop(c * piece, (c + 1) * piece, step, terms, unroll=8)
        for k in range(ROWS):
            lanes = slice(g * GROUP + k * LANES, g * GROUP + (k + 1) * LANES)
            out_ref[0, :, lanes] = rows[pl.ds(k * pitch, length), :].astype(bf16)


def whole_kernel(order, length, pitch, total, odd, inputs, taps, gate, edge, rates, scaled, skip, start, out_ref,
                 raw, rows, mode_rows, start_rows):
    steps = [jnp.exp(-(rate / total)) for rate in by_mode(mode_rows, rates[0], order)]
    scales = by_mode(mode_rows, scaled[...], order)
    start_rows[...] = start[...].astype(f32)
    at = pl.ds(odd * ROWS, ROWS)
    weights = [taps[a] for a in range(TAPS)]
    for k in range(ROWS):
        raw[pl.ds(k * pitch, length), :] = inputs[0, 0, :, k * LANES : (k + 1) * LANES].astype(f32)

    def lead_step(pair, before):
        for sub in range(2):
            t = 2 * pair + sub
            one, two = before
            now = raw[pl.ds(t, ROWS, stride=pitch), :]
            rows[pl.ds(t, ROWS, stride=pitch), :] = weights[0] * now + weights[1] * one + weights[2] * two
            before = (now, one)
        return before

    lax.fori_loop(0, length // 2, lead_step, (edge[1], edge[0]), unroll=4)

    def tokens(pair, states, both):
        for sub, gated in enumerate(both):
            t = 2 * pair + sub
            states = tuple(s * x + gated for s, x in zip(steps, states))
            mixed = tree_sum([w * x for w, x in zip(scales, states)]) + skip[...] * gated
            raw[pl.ds(t, ROWS, stride=pitch), :] = rows[pl.ds(t, ROWS, stride=pitch), :] * mixed
        return states

    def step(pair, states):
        both = gate[0, pair].astype(f32)
        return tokens(pair, states, (both[:ROWS], both[ROWS:]))

    states = tokens(0, tuple(start_rows[n, at, :] for n in range(order)), (edge[2], edge[3]))
    lax.fori_loop(1, length // 2, step, states, unroll=3)
    for k in range(ROWS):
        out_ref[0, :, pl.ds(k * LANES, LANES)] = raw[pl.ds(k * pitch, length), :].astype(bf16)


def place_kernel(part, *rest):
    rest[-1][...] = part[...]


def scan_kernel(came, span, enter):
    keep = jnp.exp(-span[lax.axis_index("seq")])
    state = jnp.zeros(keep.shape, f32)
    for j in range(came.shape[0]):
        enter[j] = state.astype(bf16)
        state = keep * state + came[j].astype(f32)


def after(*arrays):
    return lax.optimization_barrier(arrays)


def call(body, name, groups, ops, length, in_specs, out_specs, out_shape, scratch, aliases={}):
    return pl.pallas_call(
        body,
        grid=(groups,),
        in_specs=in_specs,
        out_specs=out_specs,
        out_shape=out_shape,
        scratch_shapes=scratch,
        input_output_aliases=aliases,
        compiler_params=pltpu.CompilerParams(vmem_limit_bytes=16 << 20),
        cost_estimate=pl.CostEstimate(
            flops=ops * length * groups * GROUP, bytes_accessed=8 * length * groups * GROUP, transcendentals=0
        ),
        name=name,
    )


def shards(projected, short_filter, decay_rate, residue, skip_gain):
    length, width = projected.shape[2:]
    order = decay_rate.shape[1]
    nseq = lax.axis_size("seq")
    sections = lax.axis_size("pipe")
    total = length * nseq
    groups = width // GROUP
    tiles = width // LANES
    pitch = length + 9
    onward = [(i, i + 1) for i in range(sections - 1)]
    held = lambda x: pltpu.with_memory_space_constraint(x, pltpu.HBM)
    to_all = lambda x: lax.all_to_all(x, "seq", 0, 0, tiled=True)
    taps = short_filter.reshape(3 * TAPS, tiles, LANES)
    skip = skip_gain.reshape(tiles, LANES)
    rim = lax.ppermute(projected[:, :, length - (TAPS - 1) :, :], "seq", [(i, i + 1) for i in range(nseq - 1)])

    tokens = lambda at: pl.BlockSpec((1, length, ROWS, LANES), lambda g: (at + g, 0, 0, 0))
    pairs = lambda at: pl.BlockSpec((1, length // 2, 2 * ROWS, LANES), lambda g: (at + g, 0, 0, 0))
    stack = lambda n, at: pl.BlockSpec((n, ROWS, LANES), lambda g: (0, at + g, 0))
    rate_block = lambda at: pl.BlockSpec((1, order, GROUP), lambda g: (0, 0, at + g))
    scale_block = lambda at: pl.BlockSpec((order, GROUP), lambda g: (0, at + g))
    out_block = lambda at: pl.BlockSpec((1, length, GROUP), lambda g: (0, 0, at + g))
    anywhere = pl.BlockSpec(memory_space=pl.ANY)
    shape = lambda *dims: jax.ShapeDtypeStruct(dims, f32)
    mode_rows = pltpu.VMEM((ROWS * order, LANES), f32)
    ends, span, head, gate = pl.pallas_call(
        functools.partial(state_kernel, order, length, pitch, total),
        in_specs=[anywhere] * 3,
        out_shape=[
            shape(order, tiles, LANES), shape(order, tiles, LANES), shape(4, tiles, LANES),
            jax.ShapeDtypeStruct((groups, length // 2, 2 * ROWS, LANES), bf16),
        ],
        scratch_shapes=[
            pltpu.VMEM((groups, 2, length, GROUP), bf16),
            pltpu.VMEM((3 * TAPS, tiles, LANES), f32),
            pltpu.VMEM((order, width), f32),
            pltpu.VMEM((2, ROWS * pitch, LANES), f32),
            mode_rows,
            pltpu.SemaphoreType.DMA((groups + 2,)),
        ],
        compiler_params=pltpu.CompilerParams(vmem_limit_bytes=16 << 20),
        cost_estimate=pl.CostEstimate(flops=55 * length * width, bytes_accessed=8 * length * width, transcendentals=0),
        name="local_states",
    )(held(projected), held(taps), held(decay_rate))
    wire, edge = pl.pallas_call(
        functools.partial(patch_kernel, order, length),
        out_shape=[jax.ShapeDtypeStruct((order, tiles, LANES), bf16), shape(4, tiles, LANES)],
        scratch_shapes=[pltpu.VMEM((6, tiles, LANES), f32)],
        compiler_params=pltpu.CompilerParams(vmem_limit_bytes=8 << 20),
        name="first_tokens",
    )(rim, head, taps, ends, span)

    def local_mix(at, gated):
        return call(
            functools.partial(mix_kernel, order, length, pitch, total), "local_mix", EARLY, 80, length,
            [pl.BlockSpec((1, 1, length, GROUP), lambda g: (0, 0, 0, at + g)), stack(TAPS, at),
             pairs(at), stack(4, at), rate_block(at), scale_block(at),
             pl.BlockSpec((ROWS, LANES), lambda g: (at + g, 0))],
            [tokens(0), tokens(0)], [pltpu.HBM((EARLY, length, ROWS, LANES), f32)] * 2,
            [pltpu.VMEM((ROWS * pitch, LANES), f32), mode_rows],
        )(held(projected), held(taps), gated, edge, held(decay_rate), scaled, held(skip))

    def packed_group(at, gated):
        return call(
            functools.partial(pack_kernel, order, length, pitch, total), "packed", 1, 80, length,
            [pl.BlockSpec((1, 1, length, GROUP), lambda g: (0, 0, 0, at)), stack(TAPS, at),
             pairs(at), stack(4, at), rate_block(at), scale_block(at),
             pl.BlockSpec((ROWS, LANES), lambda g: (at, 0))],
            pl.BlockSpec((1, packed_rows, 2 * ROWS, LANES), lambda g: (0, 0, 0, 0)),
            pltpu.HBM((1, packed_rows, 2 * ROWS, LANES), bf16),
            [pltpu.VMEM((ROWS * pitch, LANES), f32), mode_rows],
        )(held(projected), held(taps), gated, edge, held(decay_rate), scaled, held(skip))

    last = groups - 1
    packed_rows = length + 3 * order // 2
    wire, gate, residue = after(wire, gate, residue)
    scaled = residue[0] * jnp.sqrt(-jnp.expm1(-2.0 * (decay_rate[0] / total)))
    came = to_all(wire)
    packed = packed_group(last, gate)
    packed_before = lax.ppermute(packed, "pipe", onward)
    came, packed, gate, scaled = after(came, packed, gate, scaled)
    enter = pl.pallas_call(
        scan_kernel,
        out_shape=jax.ShapeDtypeStruct(came.shape, bf16),
        compiler_params=pltpu.CompilerParams(vmem_limit_bytes=4 << 20),
        name="scan_chunks",
    )(came, span)
    enter, gate = after(enter, gate)
    start = to_all(enter)
    mixes = local_mix(0, gate)
    start, mixes, gate = after(start, mixes, gate)
    scale_tile = scaled[:, last * GROUP :].reshape(order, ROWS, LANES)
    sent = (start[:, last * ROWS :].astype(f32) * scale_tile).astype(bf16)
    start_before = lax.ppermute(sent, "pipe", onward).astype(f32)
    in_vmem = pl.BlockSpec(memory_space=pltpu.VMEM)
    share = jax.ShapeDtypeStruct((1, length, GROUP), bf16)
    handed = None
    for at in range(last):
        if at < EARLY:
            output = pl.pallas_call(
                functools.partial(finish_kernel, order, length, pitch, total, at, 1),
                in_specs=[anywhere] * 2 + [in_vmem] * 3,
                out_specs=in_vmem,
                out_shape=share,
                scratch_shapes=[
                    pltpu.VMEM((2, length, ROWS, LANES), f32),
                    pltpu.VMEM((ROWS * pitch, LANES), f32),
                    mode_rows,
                    pltpu.SemaphoreType.DMA((2, PIECES)),
                ],
                compiler_params=pltpu.CompilerParams(vmem_limit_bytes=16 << 20),
                cost_estimate=pl.CostEstimate(
                    flops=(40 if at else FIRST_OPS) * length * GROUP, bytes_accessed=8 * length * GROUP, transcendentals=0
                ),
                name="finished",
            )(*map(held, mixes), decay_rate, scaled, start)
        else:
            output = call(
                functools.partial(whole_kernel, order, length, pitch, total, at % 2), "mixed_output", 1, 90, length,
                [pl.BlockSpec((1, 1, length, GROUP), lambda g, at=at: (0, 0, 0, at)), stack(TAPS, at),
                 pairs(at), stack(4, at), rate_block(at), scale_block(at),
                 pl.BlockSpec((ROWS, LANES), lambda g, at=at: (at, 0)),
                 pl.BlockSpec((order, 2 * ROWS, LANES), lambda g, at=at: (0, at // 2, 0))],
                out_block(0), share,
                [pltpu.VMEM((ROWS * pitch, LANES), f32)] * 2
                + [mode_rows, pltpu.VMEM((order, 2 * ROWS, LANES), f32)],
            )(held(projected), held(taps), gate, edge, held(decay_rate), scaled, held(skip), start)
        if at == 0:
            output, packed_before = after(output, packed_before)
        came = lax.ppermute(output, "pipe", onward)
        given = [came] if handed is None else [came, handed]
        handed = call(
            place_kernel, "placed", 1, PLACE_OPS, length, [out_block(0)] + [anywhere] * (len(given) - 1),
            out_block(at), jax.ShapeDtypeStruct((1, length, width), bf16), [], {1: 0} if len(given) > 1 else {},
        )(*given)
        if at == UNPACK:
            handed = call(
                functools.partial(unpack_kernel, order, length, pitch, total), "finished_ahead", 1, PLACE_OPS, length,
                [pl.BlockSpec((1, packed_rows, 2 * ROWS, LANES), lambda g: (0, 0, 0, 0)), stack(order, 0), anywhere],
                out_block(last), jax.ShapeDtypeStruct((1, length, width), bf16),
                [pltpu.VMEM((ROWS * pitch, LANES), f32)], {2: 0},
            )(packed_before, start_before, handed)
    return handed


def solution(mesh):
    in_specs = (
        P("pipe", None, "seq", None),
        P("pipe", None, None, None),
        P("pipe", None, None),
        P("pipe", None, None),
        P("pipe", None),
    )
    out_specs = P("pipe", "seq", None)
    return jax.shard_map(shards, mesh=mesh, in_specs=in_specs, out_specs=out_specs, check_vma=False)
```
